32 devices in a mesh: rep: 4 (over y, x), shard: 8 (over z, core).
Axes of the slice: x: 2, y: 2, z: 4, core: 2. Of those that a mesh axis runs over, the one named last changes fastest.
Arguments:
- queries: bfloat16 [4, 1024, 256], P('rep', 'shard'), may hold values from -64 to 64
- targets: int32 [4, 1024], P('rep', 'shard'), may hold values from 0 to 4095, as said below
- samp_ids: int32 [4, 32], P('rep', 'shard'), may hold values from 0 to 5, as said below
- counts: int32 [4, 8], P('rep', 'shard'), may hold values from 1 to 4, as said below
- logq: float32 [4, 32], P('rep', 'shard'), may hold values from -9 to -5
- table: float32 [6144, 256], P('shard'), may hold values from -1 to 1
- first_moment: float32 [6144, 256], P('shard'), may hold values from -2 to 2
- second_moment: float32 [6144, 256], P('shard'), may hold values from 0.01 to 1
Outputs:
- loss: float32 [4, 1024], P('rep', 'shard')
- query_grad: float32 [4, 1024, 256], P('rep', 'shard')
- new_table: float32 [6144, 256], P('shard')
- new_first: float32 [6144, 256], P('shard')
- new_second: float32 [6144, 256], P('shard')
The draws below stay inside these ranges and needn't reach their ends.
Inputs may be any that keep to these rules, and one draw needn't show every extreme that they name: In each group some device counts 4; when a device counts 4, the device of its group whose shard index differs in the lowest bit counts at most 2. `samp_ids`: the 4 numbers listed for one device are distinct. `targets`: the slot always lies in a live block of the query's group.
All inputs are finite; a program needn't handle non-finite values.
Results may differ from the reference program's by a relative error of at most 0.0085.
Values may be sent and summed in bfloat16 or wider, within the bound.
A program may use at most 64 MiB of HBM per device.

```python
import math
import jax
import jax.numpy as jnp
from jax import lax

D = 256
BLOCK = 128
BLK_DEV = 6
SAMP_DEV = 4
QUERIES = 1024
SLOTS = 32
ITEMS = 6144
N_REP = 4
N_SHARD = 8


def full_device():
    return (N_SHARD - 1 - jnp.arange(N_REP, dtype=jnp.int32) % N_SHARD).astype(jnp.int32)


def sample_plan(key):
    base = jax.random.fold_in(key, 7001)
    high_key, low_key, flip_key, order_key = jax.random.split(base, 4)
    pair_count = N_SHARD // 2
    high = jax.random.randint(high_key, (N_REP, pair_count), 1, SAMP_DEV + 1)
    low = jax.random.randint(low_key, (N_REP, pair_count), 1, SAMP_DEV - 1)
    flip = jax.random.randint(flip_key, (N_REP, pair_count), 0, 2)
    full_dev = full_device()
    full_pair = jnp.arange(pair_count, dtype=jnp.int32)[None, :] == (full_dev // 2)[:, None]
    high = jnp.where(full_pair, SAMP_DEV, high)
    flip = jnp.where(full_pair, (full_dev % 2)[:, None], flip)
    even_count = jnp.where(flip == 0, high, low)
    odd_count = jnp.where(flip == 0, low, high)
    block_counts = jnp.stack([even_count, odd_count], axis=-1).reshape(N_REP, N_SHARD).astype(jnp.int32)
    raw = jax.random.randint(order_key, (N_REP, N_SHARD, BLK_DEV), 0, 1 << 20)
    ranked = raw * BLK_DEV + jnp.arange(BLK_DEV, dtype=jnp.int32)
    order = jnp.argsort(ranked, axis=-1, stable=True)[..., :SAMP_DEV]
    return (block_counts, order.reshape(N_REP, SLOTS).astype(jnp.int32))


def table_values(key):
    return jax.random.normal(jax.random.fold_in(key, 7003), (ITEMS, D), jnp.float32) / math.sqrt(D)


def draw_table(key, part):
    return jnp.clip(table_values(key), -1.0, 1.0)


def draw_counts(key, part):
    return sample_plan(key)[0]


def draw_samp_ids(key, part):
    return sample_plan(key)[1]


def draw_targets(key, part):
    block_counts, order = sample_plan(key)
    first_key, second_key, third_key = jax.random.split(jax.random.fold_in(key, 7002), 3)
    owner = jax.random.randint(first_key, (N_REP, QUERIES), 0, N_SHARD)
    raw = jax.random.randint(second_key, (N_REP, QUERIES), 0, 1 << 16)
    own_count = jnp.take_along_axis(block_counts, owner, axis=1)
    block = raw % own_count
    item = jax.random.randint(third_key, (N_REP, QUERIES), 0, BLOCK)
    picked = (owner * (SAMP_DEV * BLOCK) + block * BLOCK + item).astype(jnp.int32)
    picked = picked.at[0, 0].set(SLOTS * BLOCK - 1)
    picked = picked.at[0, 1].set(0)
    return picked.astype(jnp.int32)


def draw_queries(key, part):
    values = jax.random.normal(jax.random.fold_in(key, 7004), (N_REP, QUERIES, D), jnp.float32)
    return jnp.clip(values, -64.0, 64.0).astype(jnp.bfloat16)


def block_scale(key, dims, cuts, least, high):
    gain = 1.0
    for dim, shards_of in cuts:
        heights = jax.random.uniform(jax.random.fold_in(jax.random.fold_in(key, 6), dim), (shards_of,), jnp.float32, least / len(cuts), high / len(cuts))
        gain = gain * jnp.repeat(jnp.exp(heights), dims[dim] // shards_of).reshape((-1,) + (1,) * (len(dims) - 1 - dim))
    return gain


def scatter_about(rng, extent, spread, most, cuts=(), held_as=jnp.bfloat16):
    entries = jax.random.normal(rng, extent, jnp.float32) * spread
    if len(cuts) > 0:
        entries = block_scale(rng, extent, cuts, -0.22, 0.18) * entries
    return jnp.clip(entries, min=-most, max=most).astype(held_as)


def setup_inputs(seed: int = 0) -> dict:
    key_list = jax.random.split(jax.random.key(seed), 9)
    return {
        "queries": draw_queries(jax.random.fold_in(key_list[8], 71), 0),
        "targets": draw_targets(jax.random.fold_in(key_list[8], 71), 0),
        "samp_ids": draw_samp_ids(jax.random.fold_in(key_list[8], 71), 0),
        "counts": draw_counts(jax.random.fold_in(key_list[8], 71), 0),
        "logq": jnp.clip(-9.0 + 4.0 * jax.random.uniform(key_list[4], (N_REP, SLOTS), jnp.float32) ** block_scale(key_list[4], (N_REP, SLOTS), ((0, 4), (1, 8)), -0.2, 0.2), -9.0, -5.0),
        "table": draw_table(jax.random.fold_in(key_list[8], 71), 0),
        "first_moment": scatter_about(key_list[6], (ITEMS, D), 0.3, 2.0, ((0, 8),), jnp.float32),
        "second_moment": jnp.clip(jnp.exp(math.log(1.0) - 4.6051702 * jax.random.uniform(key_list[7], (ITEMS, D), jnp.float32) ** block_scale(key_list[7], (ITEMS, D), ((0, 8),), -0.2, 0.2)), 0.01, 1.0),
    }


logit_scale = 2.0
beta_first = 0.9
beta_second = 0.99
learn_rate = 0.01
adam_eps = 1e-08
bias_first = 1.0 - 0.9 ** 10
bias_second = 1.0 - 0.99 ** 10
floor_value = -1e+30

def candidate_rows(group_ids):
    owner = jnp.arange(SLOTS, dtype=jnp.int32) // SAMP_DEV
    start = owner * (BLK_DEV * BLOCK) + group_ids.astype(jnp.int32) * BLOCK
    rows = start[:, None] + jnp.arange(BLOCK, dtype=jnp.int32)[None, :]
    return rows.reshape(-1)

def group_terms(table_half, group_queries, group_targets, group_ids, group_counts, group_logq):
    rows = candidate_rows(group_ids)
    items = table_half[rows]
    slot_live = jnp.arange(SLOTS, dtype=jnp.int32) % SAMP_DEV < jnp.repeat(group_counts, SAMP_DEV)
    live = jnp.repeat(slot_live, BLOCK)
    shift = jnp.repeat(group_logq, BLOCK)
    scores = logit_scale * jnp.dot(group_queries, items.T, preferred_element_type=jnp.float32) - shift[None, :]
    masked = jnp.where(live[None, :], scores, floor_value)
    top = lax.optimization_barrier(jnp.max(masked, axis=1))
    sums = lax.optimization_barrier(jnp.sum(jnp.where(live[None, :], jnp.exp(masked - top[:, None]), 0.0), axis=1))
    norm_total = top + jnp.log(sums)
    chosen = jnp.take_along_axis(scores, group_targets[:, None].astype(jnp.int32), axis=1)[:, 0]
    loss = norm_total - chosen
    onehot = (jnp.arange(SLOTS * BLOCK, dtype=jnp.int32)[None, :] == group_targets[:, None]).astype(jnp.float32)
    probs = jnp.where(live[None, :], jnp.exp(masked - norm_total[:, None]), 0.0)
    dlogit = (probs - onehot).astype(jnp.bfloat16)
    item_part = logit_scale * jnp.dot(dlogit.T, group_queries, preferred_element_type=jnp.float32)
    query_grad = logit_scale * jnp.dot(dlogit, items, preferred_element_type=jnp.float32)
    dense = jnp.zeros((ITEMS, D), jnp.float32).at[rows].add(item_part)
    return (loss, query_grad, dense)

def reference(queries, targets, samp_ids, counts, logq, table, first_moment, second_moment):
    table_half = table.astype(jnp.bfloat16)

    def one_group(carry, inputs):
        group_queries, group_targets, group_ids, group_counts, group_logq = inputs
        loss, query_grad, dense = group_terms(table_half, group_queries, group_targets, group_ids, group_counts, group_logq)
        return (carry + dense, (loss, query_grad))
    item_grad, outputs = lax.scan(one_group, jnp.zeros((ITEMS, D), jnp.float32), (queries, targets, samp_ids, counts, logq))
    loss, query_grad = outputs
    new_first = beta_first * first_moment + (1.0 - beta_first) * item_grad
    new_second = beta_second * second_moment + (1.0 - beta_second) * item_grad * item_grad
    new_table = table - learn_rate * (new_first / bias_first) / (jnp.sqrt(new_second / bias_second) + adam_eps)
    return (loss, query_grad, new_table, new_first, new_second)
```

```python
import functools

import jax
import jax.numpy as jnp
from jax import lax
from jax.experimental import pallas as pl
from jax.experimental.pallas import tpu as pltpu
from jax.sharding import PartitionSpec as P

BLOCK = 128
MESH = pl.DeviceIdType.MESH

logit_scale = 2.0
beta_first = 0.9
beta_second = 0.99
learn_rate = 0.01
adam_eps = 1e-08
bias_first = 1.0 - 0.9**10
bias_second = 1.0 - 0.99**10
dead_shift = 1e30


def adam_update(weights, first, second, gradient):
    first = beta_first * first + (1.0 - beta_first) * gradient
    second = beta_second * second + (1.0 - beta_second) * gradient * gradient
    weights = weights - learn_rate * (first / bias_first) / (
        jnp.sqrt(second / bias_second) + adam_eps
    )
    return (weights, first, second)


def pick_kernel(slots, blocks, ids_ref, counts_ref, logq_ref, table_ref, mine_ref, shift_ref, place_ref):
    count = counts_ref[0, 0]
    for j in range(slots):
        number = ids_ref[0, j]
        start = pl.multiple_of(number * BLOCK, BLOCK)
        mine_ref[pl.ds(j * BLOCK, BLOCK), :] = table_ref[pl.ds(start, BLOCK), :].astype(jnp.bfloat16)
        shift_ref[j] = jnp.full(shift_ref.shape[1:], jnp.where(j < count, logq_ref[0, j], dead_shift), jnp.float32)
        for b in range(blocks):
            place_ref[b, j] = jnp.full(place_ref.shape[2:], jnp.where(number == b, 1.0, 0.0), jnp.float32)


def kernel(
    n_rep, n_col, slots, blocks,
    targets_ref, queries_ref, mine_ref, shift_ref, place_ref,
    loss_ref, qgrad_ref, grad_ref,
    q_all, t_all, items, items_t, shifts, scores, dlog, stats, norm, pick_own, pick_all,
    part_own, part_out, part_in, qg_own, qg_out, qg_in, bf_out, bf_in,
    q_send, q_recv, t_send, t_recv, it_send, it_recv, st_send, st_recv, pk_send, pk_recv,
    gp_send, gp_recv, qg_send, qg_recv, bf_send, bf_recv,
):
    rep = lax.axis_index("rep")
    shard = lax.axis_index("shard")
    col = shard // 2
    core = shard % 2
    rows = queries_ref.shape[1]
    width = queries_ref.shape[2]
    half_width = width // 2
    half = slots * BLOCK
    bits = n_rep.bit_length() - 1
    sibling = {"rep": rep, "shard": col * 2 + (1 - core)}
    other = 1 - core

    def column(c):
        return {"rep": rep, "shard": c * 2 + core}

    def flipped(bit):
        size = 1 << bit
        return {"rep": rep + size * (1 - 2 * ((rep // size) % 2)), "shard": shard}

    def remote(src, dst, send, recv, device):
        return pltpu.make_async_remote_copy(
            src_ref=src, dst_ref=dst, send_sem=send, recv_sem=recv, device_id=device, device_id_type=MESH
        )

    barrier = pltpu.get_barrier_semaphore()
    for step in range(1, n_col):
        pl.semaphore_signal(barrier, inc=1, device_id=column((col + step) % n_col), device_id_type=MESH)
    pl.semaphore_signal(barrier, inc=1, device_id=sibling, device_id_type=MESH)
    for bit in range(bits):
        pl.semaphore_signal(barrier, inc=1, device_id=flipped(bit), device_id_type=MESH)
    t_all[col] = jnp.broadcast_to(targets_ref[...], (8, rows))
    q_all[col] = queries_ref[0]
    items[core] = mine_ref[...]
    shifts[core] = shift_ref[...]
    pl.semaphore_wait(barrier, n_col + bits)

    for step in range(1, n_col):
        c = (col + step) % n_col
        remote(queries_ref.at[0], q_all.at[col], q_send.at[c], q_recv.at[col], column(c)).start()
        remote(t_all.at[col], t_all.at[col], t_send.at[c], t_recv.at[col], column(c)).start()

    remote(items.at[core], items.at[core], it_send.at[0], it_recv.at[0], sibling).start()
    remote(shifts.at[core], shifts.at[core], it_send.at[1], it_recv.at[1], sibling).start()
    remote(items.at[other], items.at[other], it_send.at[0], it_recv.at[0], sibling).wait_recv()
    remote(shifts.at[other], shifts.at[other], it_send.at[1], it_recv.at[1], sibling).wait_recv()
    for side in range(2):
        items_t[:, pl.ds(side * half, half)] = items[side].T

    row_ids = lax.broadcasted_iota(jnp.int32, (half, rows), 0)
    base = col * (2 * half)

    def score_chunk(c):
        tops = []
        picks = []
        for side in range(2):
            product = lax.dot_general(
                items[side], q_all[c], (((1,), (1,)), ((), ())), preferred_element_type=jnp.float32
            )
            shift = shifts[side][:, None, :, :]
            value = (logit_scale * product).reshape(slots, BLOCK // 8, 8, rows) - shift
            value = value.reshape(half, rows)
            scores[c, side] = value
            marked = row_ids == t_all[c][0:1, :] - (base + side * half)
            tops.append(jnp.max(value, axis=0, keepdims=True))
            picks.append(jnp.sum(jnp.where(marked, value, 0.0), axis=0, keepdims=True))
        top = jnp.maximum(tops[0], tops[1])
        total = jnp.zeros((1, rows), jnp.float32)
        for side in range(2):
            total = total + jnp.sum(jnp.exp(scores[c, side] - top), axis=0, keepdims=True)
        stats[col, pl.ds(c, 1), :] = top
        stats[col, pl.ds(n_col + c, 1), :] = total
        pick_own[c] = jnp.broadcast_to(picks[0] + picks[1], (8, rows))

    score_chunk(col)

    @pl.loop(1, n_col)
    def _(step):
        c = (col + step) % n_col
        remote(q_all.at[c], q_all.at[c], q_send.at[c], q_recv.at[c], sibling).wait_recv()
        remote(t_all.at[c], t_all.at[c], t_send.at[c], t_recv.at[c], sibling).wait_recv()
        score_chunk(c)

    for step in range(1, n_col):
        c = (col + step) % n_col
        remote(stats.at[col], stats.at[col], st_send.at[c], st_recv.at[col], column(c)).start()
    for step in range(1, n_col):
        c = (col + step) % n_col
        remote(pick_own.at[c], pick_all.at[col], pk_send.at[c], pk_recv.at[col], column(c)).start()
    for step in range(1, n_col):
        c = (col + step) % n_col
        remote(stats.at[c], stats.at[c], st_send.at[c], st_recv.at[c], sibling).wait_recv()

    top = stats[0, 0:n_col, :]
    for c in range(1, n_col):
        top = jnp.maximum(top, stats[c, 0:n_col, :])
    total = jnp.zeros_like(top)
    for c in range(n_col):
        total = total + stats[c, n_col : 2 * n_col, :] * jnp.exp(stats[c, 0:n_col, :] - top)
    norm[...] = top + jnp.log(total)

    every_query = q_all[...].reshape(n_col * rows, width)

    def item_part(side):
        @pl.loop(0, n_col)
        def _(c):
            marked = row_ids == t_all[c][0:1, :] - (base + side * half)
            probs = jnp.exp(scores[c, side] - norm[pl.ds(c, 1), :])
            value = (probs - marked.astype(jnp.float32)).astype(jnp.bfloat16)
            dlog[side, :, pl.ds(pl.multiple_of(c * rows, rows), rows)] = value

        return logit_scale * jnp.dot(dlog[side], every_query, preferred_element_type=jnp.float32)

    part_out[...] = item_part(other).astype(jnp.bfloat16)
    to_sibling = remote(
        part_out, part_in, gp_send, gp_recv, sibling
    )
    to_sibling.start()
    part_own[...] = item_part(core)

    def query_part(c):
        lanes = pl.ds(pl.multiple_of(c * rows, rows), rows)
        value = jnp.dot(items_t[:, pl.ds(0, half)], dlog[0, :, lanes], preferred_element_type=jnp.float32)
        value += jnp.dot(items_t[:, pl.ds(half, half)], dlog[1, :, lanes], preferred_element_type=jnp.float32)
        return logit_scale * value

    @pl.loop(1, n_col)
    def _(step):
        c = (col + step) % n_col
        qg_out[c] = query_part(c).astype(jnp.bfloat16)
        remote(qg_out.at[c], qg_in.at[col], qg_send.at[c], qg_recv.at[col], column(c)).start()

    to_sibling.wait_recv()
    part_own[...] = part_own[...] + part_in[...].astype(jnp.float32)
    for b in range(blocks):
        value = jnp.zeros((BLOCK // 8, 8, width), jnp.float32)
        for j in range(slots):
            value = value + place_ref[b, j][None] * part_own[pl.ds(j * BLOCK, BLOCK), :].reshape(BLOCK // 8, 8, width)
        value = value.reshape(BLOCK, width)
        for h in range(2):
            bf_out[0, h, pl.ds(b * BLOCK, BLOCK), :] = value[:, h * half_width : (h + 1) * half_width].astype(
                jnp.bfloat16
            )

    def exchange(stage, h):
        return remote(
            bf_out.at[stage, h], bf_in.at[stage, h], bf_send.at[stage, h], bf_recv.at[stage, h],
            flipped((stage + h) % bits),
        )

    for h in range(2):
        exchange(0, h).start()

    qg_own[...] = query_part(col)
    for stage in range(bits):
        for h in range(2):
            exchange(stage, h).wait_recv()
            value = bf_out[stage, h].astype(jnp.float32) + bf_in[stage, h].astype(jnp.float32)
            if stage + 1 < bits:
                bf_out[stage + 1, h] = value.astype(jnp.bfloat16)
                exchange(stage + 1, h).start()
            else:
                grad_ref[:, h * half_width : (h + 1) * half_width] = value
        if stage == 0:
            total_qg = qg_own[...]
            picked = pick_own[col]
            for step in range(1, n_col):
                c = (col + step) % n_col
                remote(qg_in.at[c], qg_in.at[c], qg_send.at[c], qg_recv.at[c], sibling).wait_recv()
                remote(pick_all.at[c], pick_all.at[c], pk_send.at[c], pk_recv.at[c], sibling).wait_recv()
                total_qg = total_qg + qg_in[c].astype(jnp.float32)
                picked = picked + pick_all[c]
            qgrad_ref[0] = total_qg.T
            loss_ref[...] = norm[pl.ds(col, 1), :] - picked[0:1, :]

    for step in range(1, n_col):
        c = (col + step) % n_col
        remote(q_all.at[col], q_all.at[col], q_send.at[c], q_recv.at[c], sibling).wait_send()
        remote(t_all.at[col], t_all.at[col], t_send.at[c], t_recv.at[c], sibling).wait_send()
        remote(stats.at[col], stats.at[col], st_send.at[c], st_recv.at[c], sibling).wait_send()
        remote(pick_own.at[c], pick_own.at[c], pk_send.at[c], pk_recv.at[c], sibling).wait_send()
        remote(qg_out.at[c], qg_out.at[c], qg_send.at[c], qg_recv.at[c], sibling).wait_send()
    remote(items.at[core], items.at[core], it_send.at[0], it_recv.at[0], sibling).wait_send()
    remote(shifts.at[core], shifts.at[core], it_send.at[1], it_recv.at[1], sibling).wait_send()
    to_sibling.wait_send()
    for stage in range(bits):
        for h in range(2):
            exchange(stage, h).wait_send()


def local(n_rep, n_shard, queries, targets, samp_ids, counts, logq, table, first_moment, second_moment):
    rows, width = queries.shape[1:]
    slots = samp_ids.shape[1]
    items_held = table.shape[0]
    blocks = items_held // BLOCK
    n_col = n_shard // 2
    bits = n_rep.bit_length() - 1
    half = slots * BLOCK
    f32, bf16 = jnp.float32, jnp.bfloat16
    dma = pltpu.SemaphoreType.DMA
    vmem, smem = pl.BlockSpec(memory_space=pltpu.VMEM), pl.BlockSpec(memory_space=pltpu.SMEM)
    pair_flops = n_col * rows * 2 * half * width
    mine, shift, place = pl.pallas_call(
        functools.partial(pick_kernel, slots, blocks),
        out_shape=(
            jax.ShapeDtypeStruct((half, width), bf16),
            jax.ShapeDtypeStruct((slots, 8, BLOCK), f32),
            jax.ShapeDtypeStruct((blocks, slots, 8, width), f32),
        ),
        in_specs=[smem, smem, smem, vmem],
        out_specs=(vmem, vmem, vmem),
        compiler_params=pltpu.CompilerParams(vmem_limit_bytes=16 * 1024 * 1024),
    )(samp_ids, counts, logq, table)
    own_loss, query_grad, gradient = pl.pallas_call(
        functools.partial(kernel, n_rep, n_col, slots, blocks),
        out_shape=(
            jax.ShapeDtypeStruct((1, rows), f32),
            jax.ShapeDtypeStruct((1, rows, width), f32),
            jax.ShapeDtypeStruct((items_held, width), f32),
        ),
        in_specs=[vmem] * 5,
        out_specs=(vmem, vmem, vmem),
        scratch_shapes=[
            pltpu.VMEM((n_col, rows, width), bf16),
            pltpu.VMEM((n_col, 8, rows), jnp.int32),
            pltpu.VMEM((2, half, width), bf16),
            pltpu.VMEM((width, 2 * half), bf16),
            pltpu.VMEM((2, slots, 8, BLOCK), f32),
            pltpu.VMEM((n_col, 2, half, rows), f32),
            pltpu.VMEM((2, half, n_col * rows), bf16),
            pltpu.VMEM((n_col, 2 * n_col, rows), f32),
            pltpu.VMEM((n_col, rows), f32),
            pltpu.VMEM((n_col, 8, rows), f32),
            pltpu.VMEM((n_col, 8, rows), f32),
            pltpu.VMEM((half, width), f32),
            pltpu.VMEM((half, width), bf16),
            pltpu.VMEM((half, width), bf16),
            pltpu.VMEM((width, rows), f32),
            pltpu.VMEM((n_col, width, rows), bf16),
            pltpu.VMEM((n_col, width, rows), bf16),
            pltpu.VMEM((bits, 2, items_held, width // 2), bf16),
            pltpu.VMEM((bits, 2, items_held, width // 2), bf16),
            dma((n_col,)), dma((n_col,)), dma((n_col,)), dma((n_col,)),
            dma((2,)), dma((2,)),
            dma((n_col,)), dma((n_col,)), dma((n_col,)), dma((n_col,)),
            dma(()), dma(()),
            dma((n_col,)), dma((n_col,)),
            dma((bits, 2)), dma((bits, 2)),
        ],
        compiler_params=pltpu.CompilerParams(
            collective_id=0, has_side_effects=True, vmem_limit_bytes=40 * 1024 * 1024
        ),
        cost_estimate=pl.CostEstimate(
            flops=6 * pair_flops, bytes_accessed=4 * items_held * width, transcendentals=2 * pair_flops // width
        ),
    )(targets, queries, mine, shift, place)
    new_table, new_first, new_second = adam_update(table, first_moment, second_moment, gradient)
    return (own_loss, query_grad, new_table, new_first, new_second)


def solution(mesh):
    in_specs = (
        P("rep", "shard", None),
        P("rep", "shard"),
        P("rep", "shard"),
        P("rep", "shard"),
        P("rep", "shard"),
        P("shard", None),
        P("shard", None),
        P("shard", None),
    )
    out_specs = (
        P("rep", "shard"),
        P("rep", "shard", None),
        P("shard", None),
        P("shard", None),
        P("shard", None),
    )
    step = functools.partial(local, mesh.shape["rep"], mesh.shape["shard"])
    return jax.shard_map(step, mesh=mesh, in_specs=in_specs, out_specs=out_specs, check_vma=False)
```

```python
import functools

import jax
import jax.numpy as jnp
from jax import lax
from jax.experimental import pallas as pl
from jax.experimental.pallas import tpu as pltpu
from jax.sharding import PartitionSpec as P

BLOCK = 128
MESH = pl.DeviceIdType.MESH

logit_scale = 2.0
beta_first = 0.9
beta_second = 0.99
learn_rate = 0.01
adam_eps = 1e-08
bias_first = 1.0 - 0.9**10
bias_second = 1.0 - 0.99**10
dead_shift = 1e30


def adam_update(weights, first, second, gradient):
    first = beta_first * first + (1.0 - beta_first) * gradient
    second = beta_second * second + (1.0 - beta_second) * gradient * gradient
    weights = weights - learn_rate * (first / bias_first) / (
        jnp.sqrt(second / bias_second) + adam_eps
    )
    return (weights, first, second)


def kernel(
    n_rep, n_col, slots, blocks,
    ids_ref, counts_ref, logq_ref, targets_ref, queries_ref, table_ref,
    loss_ref, qgrad_ref, grad_ref,
    table_v, id_own, id_in, s_out, s_in, q_all, t_all, items, items_t, shifts, scores, dlog, stats, norm, pick_own, pick_all,
    part_own, part_out, part_in, qg_own, qg_out, qg_in, bf_out, bf_in,
    table_sem, id_send, id_recv, ss_send, ss_recv, q_send, q_recv, t_send, t_recv, it_send, it_recv, st_send, st_recv, pk_send, pk_recv,
    gp_send, gp_recv, qg_send, qg_recv, bf_send, bf_recv,
):
    rep = lax.axis_index("rep")
    shard = lax.axis_index("shard")
    col = shard // 2
    core = shard % 2
    rows = queries_ref.shape[1]
    width = queries_ref.shape[2]
    half_width = width // 2
    half = slots * BLOCK
    bits = n_rep.bit_length() - 1
    group = BLOCK * (2 if blocks % 2 == 0 else 1)
    groups = blocks * BLOCK // group
    sibling = {"rep": rep, "shard": col * 2 + (1 - core)}
    other = 1 - core

    def column(c):
        return {"rep": rep, "shard": c * 2 + core}

    def flipped(bit):
        size = 1 << bit
        return {"rep": rep + size * (1 - 2 * ((rep // size) % 2)), "shard": shard}

    def remote(src, dst, send, recv, device):
        return pltpu.make_async_remote_copy(
            src_ref=src, dst_ref=dst, send_sem=send, recv_sem=recv, device_id=device, device_id_type=MESH
        )

    load_table = pltpu.make_async_copy(table_ref, table_v, table_sem)
    load_table.start()

    barrier = pltpu.get_barrier_semaphore()
    for step in range(1, n_col):
        pl.semaphore_signal(barrier, inc=1, device_id=column((col + step) % n_col), device_id_type=MESH)
    pl.semaphore_signal(barrier, inc=1, device_id=sibling, device_id_type=MESH)
    for bit in range(bits):
        pl.semaphore_signal(barrier, inc=1, device_id=flipped(bit), device_id_type=MESH)
    t_all[col] = jnp.broadcast_to(targets_ref[...], (8, rows))
    q_all[col] = queries_ref[0]
    count = counts_ref[0, 0]
    for j in range(slots):
        shift = jnp.where(j < count, logq_ref[0, j], dead_shift)
        shifts[core, j] = jnp.full((8, BLOCK), shift, jnp.float32)
        id_own[j] = jnp.full((8, BLOCK), ids_ref[0, j].astype(jnp.float32), jnp.float32)
    pl.semaphore_wait(barrier, n_col + bits)

    for step in range(1, n_col):
        c = (col + step) % n_col
        remote(queries_ref.at[0], q_all.at[col], q_send.at[c], q_recv.at[col], column(c)).start()
        remote(t_all.at[col], t_all.at[col], t_send.at[c], t_recv.at[col], column(c)).start()

    def announce(h):
        return remote(id_own, id_in.at[h], id_send.at[h], id_recv.at[h], flipped(h % bits))

    for h in range(2):
        announce(h).start()

    def is_block(tile, b):
        return jnp.where(tile == float(b), 1.0, 0.0)[None]

    def tiles(value):
        return value.astype(jnp.float32).reshape(BLOCK // 8, 8, half_width)

    load_table.wait()
    for j in range(slots):
        for h in range(2):
            value = jnp.zeros((BLOCK // 8, 8, half_width), jnp.float32)
            for b in range(blocks):
                held = table_v[pl.ds(b * BLOCK, BLOCK), pl.ds(h * half_width, half_width)]
                value = value + is_block(id_own[j], b) * tiles(held)
            items[core, pl.ds(j * BLOCK, BLOCK), pl.ds(h * half_width, half_width)] = value.reshape(
                BLOCK, half_width
            ).astype(jnp.bfloat16)
    remote(items.at[core], items.at[core], it_send.at[0], it_recv.at[0], sibling).start()
    remote(shifts.at[core], shifts.at[core], it_send.at[1], it_recv.at[1], sibling).start()
    remote(items.at[other], items.at[other], it_send.at[0], it_recv.at[0], sibling).wait_recv()
    remote(shifts.at[other], shifts.at[other], it_send.at[1], it_recv.at[1], sibling).wait_recv()
    for side in range(2):
        items_t[:, pl.ds(side * half, half)] = items[side].T

    row_ids = lax.broadcasted_iota(jnp.int32, (half, rows), 0)
    base = col * (2 * half)

    def score_chunk(c):
        tops = []
        picks = []
        for side in range(2):
            product = lax.dot_general(
                items[side], q_all[c], (((1,), (1,)), ((), ())), preferred_element_type=jnp.float32
            )
            shift = shifts[side][:, None, :, :]
            value = (logit_scale * product).reshape(slots, BLOCK // 8, 8, rows) - shift
            value = value.reshape(half, rows)
            scores[c, side] = value
            marked = row_ids == t_all[c][0:1, :] - (base + side * half)
            tops.append(jnp.max(value, axis=0, keepdims=True))
            picks.append(jnp.sum(jnp.where(marked, value, 0.0), axis=0, keepdims=True))
        top = jnp.maximum(tops[0], tops[1])
        total = jnp.zeros((1, rows), jnp.float32)
        for side in range(2):
            total = total + jnp.sum(jnp.exp(scores[c, side] - top), axis=0, keepdims=True)
        stats[col, pl.ds(c, 1), :] = top
        stats[col, pl.ds(n_col + c, 1), :] = total
        pick_own[c] = jnp.broadcast_to(picks[0] + picks[1], (8, rows))

    score_chunk(col)

    @pl.loop(1, n_col)
    def _(step):
        c = (col + step) % n_col
        remote(q_all.at[c], q_all.at[c], q_send.at[c], q_recv.at[c], sibling).wait_recv()
        remote(t_all.at[c], t_all.at[c], t_send.at[c], t_recv.at[c], sibling).wait_recv()
        score_chunk(c)

    for step in range(1, n_col):
        c = (col + step) % n_col
        remote(stats.at[col], stats.at[col], st_send.at[c], st_recv.at[col], column(c)).start()
    for step in range(1, n_col):
        c = (col + step) % n_col
        remote(pick_own.at[c], pick_all.at[col], pk_send.at[c], pk_recv.at[col], column(c)).start()
    for step in range(1, n_col):
        c = (col + step) % n_col
        remote(stats.at[c], stats.at[c], st_send.at[c], st_recv.at[c], sibling).wait_recv()

    top = stats[0, 0:n_col, :]
    for c in range(1, n_col):
        top = jnp.maximum(top, stats[c, 0:n_col, :])
    total = jnp.zeros_like(top)
    for c in range(n_col):
        total = total + stats[c, n_col : 2 * n_col, :] * jnp.exp(stats[c, 0:n_col, :] - top)
    norm[...] = top + jnp.log(total)

    every_query = q_all[...].reshape(n_col * rows, width)

    slot_rows = lax.broadcasted_iota(jnp.int32, (BLOCK, rows), 0)

    def item_part(side, j):
        @pl.loop(0, n_col)
        def _(c):
            marked = slot_rows == t_all[c][0:1, :] - (base + side * half + j * BLOCK)
            probs = jnp.exp(scores[c, side, pl.ds(j * BLOCK, BLOCK), :] - norm[pl.ds(c, 1), :])
            value = (probs - marked.astype(jnp.float32)).astype(jnp.bfloat16)
            dlog[side, pl.ds(j * BLOCK, BLOCK), pl.ds(pl.multiple_of(c * rows, rows), rows)] = value

        return logit_scale * jnp.dot(
            dlog[side, pl.ds(j * BLOCK, BLOCK), :], every_query, preferred_element_type=jnp.float32
        )

    def to_sibling(j):
        where = pl.ds(j * BLOCK, BLOCK)
        return remote(part_out.at[where, :], part_in.at[where, :], gp_send.at[j], gp_recv.at[j], sibling)

    for j in range(slots):
        part_out[pl.ds(j * BLOCK, BLOCK), :] = item_part(other, j).astype(jnp.bfloat16)
        to_sibling(j).start()
    for j in range(slots):
        part_own[pl.ds(j * BLOCK, BLOCK), :] = item_part(core, j)

    def query_part(c):
        lanes = pl.ds(pl.multiple_of(c * rows, rows), rows)
        value = jnp.dot(items_t[:, pl.ds(0, half)], dlog[0, :, lanes], preferred_element_type=jnp.float32)
        value += jnp.dot(items_t[:, pl.ds(half, half)], dlog[1, :, lanes], preferred_element_type=jnp.float32)
        return logit_scale * value

    @pl.loop(1, n_col)
    def _(step):
        c = (col + step) % n_col
        qg_out[c] = query_part(c).astype(jnp.bfloat16)
        remote(qg_out.at[c], qg_in.at[col], qg_send.at[c], qg_recv.at[col], column(c)).start()

    def exchange_slot(h, j):
        where = pl.ds(j * BLOCK, BLOCK)
        return remote(
            s_out.at[h, where, :], s_in.at[h, where, :], ss_send.at[h, j], ss_recv.at[h, j], flipped(h % bits)
        )

    for j in range(slots):
        where = pl.ds(j * BLOCK, BLOCK)
        to_sibling(j).wait_recv()
        value = part_own[where, :] + part_in[where, :].astype(jnp.float32)
        for h in range(2):
            s_out[h, where, :] = value[:, h * half_width : (h + 1) * half_width].astype(jnp.bfloat16)
            exchange_slot(h, j).start()

    def exchange(stage, h, g):
        where = pl.ds(g * group, group)
        return remote(
            bf_out.at[stage - 1, h, where, :], bf_in.at[stage - 1, h, where, :],
            bf_send.at[stage - 1, h, g], bf_recv.at[stage - 1, h, g], flipped((stage + h) % bits),
        )

    def pass_on(stage, h, g, value):
        if stage < bits:
            bf_out[stage - 1, h, pl.ds(g * group, group), :] = value.astype(jnp.bfloat16)
            exchange(stage, h, g).start()
        else:
            grad_ref[pl.ds(g * group, group), pl.ds(h * half_width, half_width)] = value

    qg_own[...] = query_part(col)
    for h in range(2):
        announce(h).wait_recv()
        for j in range(slots):
            exchange_slot(h, j).wait_recv()
    for g in range(groups):
        for h in range(2):
            pieces = []
            for b in range(g * group // BLOCK, (g + 1) * group // BLOCK):
                mine = jnp.zeros((BLOCK // 8, 8, half_width), jnp.float32)
                theirs = mine
                for j in range(slots):
                    where = pl.ds(j * BLOCK, BLOCK)
                    mine = mine + is_block(id_own[j], b) * tiles(s_out[h, where, :])
                    theirs = theirs + is_block(id_in[h, j], b) * tiles(s_in[h, where, :])
                pieces.append((mine + theirs).reshape(BLOCK, half_width))
            pass_on(1, h, g, jnp.concatenate(pieces, axis=0))

    total_qg = qg_own[...]
    picked = pick_own[col]
    for step in range(1, n_col):
        c = (col + step) % n_col
        remote(qg_in.at[c], qg_in.at[c], qg_send.at[c], qg_recv.at[c], sibling).wait_recv()
        remote(pick_all.at[c], pick_all.at[c], pk_send.at[c], pk_recv.at[c], sibling).wait_recv()
        total_qg = total_qg + qg_in[c].astype(jnp.float32)
        picked = picked + pick_all[c]
    qgrad_ref[0] = total_qg.T
    loss_ref[...] = norm[pl.ds(col, 1), :] - picked[0:1, :]

    for stage in range(1, bits):
        for g in range(groups):
            for h in range(2):
                where = pl.ds(g * group, group)
                exchange(stage, h, g).wait_recv()
                value = bf_out[stage - 1, h, where, :].astype(jnp.float32)
                value = value + bf_in[stage - 1, h, where, :].astype(jnp.float32)
                pass_on(stage + 1, h, g, value)

    for step in range(1, n_col):
        c = (col + step) % n_col
        remote(q_all.at[col], q_all.at[col], q_send.at[c], q_recv.at[c], sibling).wait_send()
        remote(t_all.at[col], t_all.at[col], t_send.at[c], t_recv.at[c], sibling).wait_send()
        remote(stats.at[col], stats.at[col], st_send.at[c], st_recv.at[c], sibling).wait_send()
        remote(pick_own.at[c], pick_own.at[c], pk_send.at[c], pk_recv.at[c], sibling).wait_send()
        remote(qg_out.at[c], qg_out.at[c], qg_send.at[c], qg_recv.at[c], sibling).wait_send()
    remote(items.at[core], items.at[core], it_send.at[0], it_recv.at[0], sibling).wait_send()
    remote(shifts.at[core], shifts.at[core], it_send.at[1], it_recv.at[1], sibling).wait_send()
    for j in range(slots):
        to_sibling(j).wait_send()
    for h in range(2):
        announce(h).wait_send()
        for j in range(slots):
            exchange_slot(h, j).wait_send()
        for stage in range(1, bits):
            for g in range(groups):
                exchange(stage, h, g).wait_send()


def local(n_rep, n_shard, queries, targets, samp_ids, counts, logq, table, first_moment, second_moment):
    rows, width = queries.shape[1:]
    slots = samp_ids.shape[1]
    items_held = table.shape[0]
    blocks = items_held // BLOCK
    n_col = n_shard // 2
    bits = n_rep.bit_length() - 1
    half = slots * BLOCK
    f32, bf16 = jnp.float32, jnp.bfloat16
    dma = pltpu.SemaphoreType.DMA
    vmem, smem = pl.BlockSpec(memory_space=pltpu.VMEM), pl.BlockSpec(memory_space=pltpu.SMEM)
    pair_flops = n_col * rows * 2 * half * width
    own_loss, query_grad, gradient = pl.pallas_call(
        functools.partial(kernel, n_rep, n_col, slots, blocks),
        out_shape=(
            jax.ShapeDtypeStruct((1, rows), f32),
            jax.ShapeDtypeStruct((1, rows, width), f32),
            jax.ShapeDtypeStruct((items_held, width), f32),
        ),
        in_specs=[smem, smem, smem, vmem, vmem, pl.BlockSpec(memory_space=pl.ANY)],
        out_specs=(vmem, vmem, vmem),
        scratch_shapes=[
            pltpu.VMEM((items_held, width), f32),
            pltpu.VMEM((slots, 8, BLOCK), f32),
            pltpu.VMEM((2, slots, 8, BLOCK), f32),
            pltpu.VMEM((2, half, width // 2), bf16),
            pltpu.VMEM((2, half, width // 2), bf16),
            pltpu.VMEM((n_col, rows, width), bf16),
            pltpu.VMEM((n_col, 8, rows), jnp.int32),
            pltpu.VMEM((2, half, width), bf16),
            pltpu.VMEM((width, 2 * half), bf16),
            pltpu.VMEM((2, slots, 8, BLOCK), f32),
            pltpu.VMEM((n_col, 2, half, rows), f32),
            pltpu.VMEM((2, half, n_col * rows), bf16),
            pltpu.VMEM((n_col, 2 * n_col, rows), f32),
            pltpu.VMEM((n_col, rows), f32),
            pltpu.VMEM((n_col, 8, rows), f32),
            pltpu.VMEM((n_col, 8, rows), f32),
            pltpu.VMEM((half, width), f32),
            pltpu.VMEM((half, width), bf16),
            pltpu.VMEM((half, width), bf16),
            pltpu.VMEM((width, rows), f32),
            pltpu.VMEM((n_col, width, rows), bf16),
            pltpu.VMEM((n_col, width, rows), bf16),
            pltpu.VMEM((max(bits - 1, 1), 2, items_held, width // 2), bf16),
            pltpu.VMEM((max(bits - 1, 1), 2, items_held, width // 2), bf16),
            dma(()), dma((2,)), dma((2,)), dma((2, slots)), dma((2, slots)),
            dma((n_col,)), dma((n_col,)), dma((n_col,)), dma((n_col,)),
            dma((2,)), dma((2,)),
            dma((n_col,)), dma((n_col,)), dma((n_col,)), dma((n_col,)),
            dma((slots,)), dma((slots,)),
            dma((n_col,)), dma((n_col,)),
            dma((bits, 2, blocks)), dma((bits, 2, blocks)),
        ],
        compiler_params=pltpu.CompilerParams(
            collective_id=0, has_side_effects=True, vmem_limit_bytes=40 * 1024 * 1024
        ),
        cost_estimate=pl.CostEstimate(
            flops=6 * pair_flops, bytes_accessed=4 * items_held * width, transcendentals=2 * pair_flops // width
        ),
    )(samp_ids, counts, logq, targets, queries, table)
    new_table, new_first, new_second = adam_update(table, first_moment, second_moment, gradient)
    return (own_loss, query_grad, new_table, new_first, new_second)


def solution(mesh):
    in_specs = (
        P("rep", "shard", None),
        P("rep", "shard"),
        P("rep", "shard"),
        P("rep", "shard"),
        P("rep", "shard"),
        P("shard", None),
        P("shard", None),
        P("shard", None),
    )
    out_specs = (
        P("rep", "shard"),
        P("rep", "shard", None),
        P("shard", None),
        P("shard", None),
        P("shard", None),
    )
    step = functools.partial(local, mesh.shape["rep"], mesh.shape["shard"])
    return jax.shard_map(step, mesh=mesh, in_specs=in_specs, out_specs=out_specs, check_vma=False)
```

```python
import functools

import jax
import jax.numpy as jnp
from jax import lax
from jax.experimental import pallas as pl
from jax.experimental.pallas import tpu as pltpu
from jax.sharding import PartitionSpec as P

BLOCK = 128
MESH = pl.DeviceIdType.MESH

logit_scale = 2.0
beta_first = 0.9
beta_second = 0.99
learn_rate = 0.01
adam_eps = 1e-08
bias_first = 1.0 - 0.9**10
bias_second = 1.0 - 0.99**10
dead_shift = 1e30


def adam_update(weights, first, second, gradient):
    first = beta_first * first + (1.0 - beta_first) * gradient
    second = beta_second * second + (1.0 - beta_second) * gradient * gradient
    weights = weights - learn_rate * (first / bias_first) / (
        jnp.sqrt(second / bias_second) + adam_eps
    )
    return (weights, first, second)


def kernel(
    n_rep, n_col, slots, blocks,
    ids_hbm, counts_hbm, logq_hbm, targets_hbm, queries_ref, table_ref,
    loss_ref, qgrad_ref, grad_ref,
    ids_ref, counts_ref, logq_ref, targets_ref, table_v, id_own, id_in, s_out, s_in, q_all, t_all, items, items_t, shifts, scores, dlog, stats, norm, pick_own, pick_all,
    part_own, part_out, part_in, qg_own, qg_out, qg_in, bf_out, bf_in,
    small_sem, own_sem, table_sem, id_send, id_recv, ss_send, ss_recv, q_send, q_recv, t_send, t_recv, it_send, it_recv, st_send, st_recv, pk_send, pk_recv,
    gp_send, gp_recv, qg_send, qg_recv, bf_send, bf_recv,
):
    rep = lax.axis_index("rep")
    shard = lax.axis_index("shard")
    col = shard // 2
    core = shard % 2
    rows = queries_ref.shape[1]
    width = queries_ref.shape[2]
    half_width = width // 2
    half = slots * BLOCK
    bits = n_rep.bit_length() - 1
    group = BLOCK * (2 if blocks % 2 == 0 else 1)
    groups = blocks * BLOCK // group
    sibling = {"rep": rep, "shard": col * 2 + (1 - core)}
    other = 1 - core

    def column(c):
        return {"rep": rep, "shard": c * 2 + core}

    def flipped(bit):
        size = 1 << bit
        return {"rep": rep + size * (1 - 2 * ((rep // size) % 2)), "shard": shard}

    def remote(src, dst, send, recv, device):
        return pltpu.make_async_remote_copy(
            src_ref=src, dst_ref=dst, send_sem=send, recv_sem=recv, device_id=device, device_id_type=MESH
        )

    load_table = pltpu.make_async_copy(table_ref, table_v, table_sem)
    load_small = [
        pltpu.make_async_copy(src, dst, small_sem.at[i])
        for i, (src, dst) in enumerate(
            [(ids_hbm, ids_ref), (counts_hbm, counts_ref), (logq_hbm, logq_ref), (targets_hbm, targets_ref)]
        )
    ]
    load_own = pltpu.make_async_copy(queries_ref.at[0], q_all.at[col], own_sem)
    for load in load_small:
        load.start()
    load_own.start()
    load_table.start()

    barrier = pltpu.get_barrier_semaphore()
    for step in range(1, n_col):
        pl.semaphore_signal(barrier, inc=1, device_id=column((col + step) % n_col), device_id_type=MESH)
    pl.semaphore_signal(barrier, inc=1, device_id=sibling, device_id_type=MESH)
    for bit in range(bits):
        pl.semaphore_signal(barrier, inc=1, device_id=flipped(bit), device_id_type=MESH)
    for load in load_small:
        load.wait()
    t_all[col] = jnp.broadcast_to(targets_ref[...], (8, rows))
    count = counts_ref[0, 0]
    for j in range(slots):
        shift = jnp.where(j < count, logq_ref[0, j], dead_shift)
        shifts[core, j] = jnp.full((8, BLOCK), shift, jnp.float32)
        id_own[j] = jnp.full((8, BLOCK), ids_ref[0, j].astype(jnp.float32), jnp.float32)
    pl.semaphore_wait(barrier, n_col + bits)

    for step in range(1, n_col):
        c = (col + step) % n_col
        remote(queries_ref.at[0], q_all.at[col], q_send.at[c], q_recv.at[col], column(c)).start()
        remote(t_all.at[col], t_all.at[col], t_send.at[c], t_recv.at[col], column(c)).start()

    def announce(h):
        return remote(id_own, id_in.at[h], id_send.at[h], id_recv.at[h], flipped(h % bits))

    for h in range(2):
        announce(h).start()

    def is_block(tile, b):
        return jnp.where(tile == float(b), 1.0, 0.0)[None]

    def tiles(value):
        return value.astype(jnp.float32).reshape(BLOCK // 8, 8, half_width)

    load_table.wait()
    for j in range(slots):
        for h in range(2):
            value = jnp.zeros((BLOCK // 8, 8, half_width), jnp.float32)
            for b in range(blocks):
                held = table_v[pl.ds(b * BLOCK, BLOCK), pl.ds(h * half_width, half_width)]
                value = value + is_block(id_own[j], b) * tiles(held)
            items[core, pl.ds(j * BLOCK, BLOCK), pl.ds(h * half_width, half_width)] = value.reshape(
                BLOCK, half_width
            ).astype(jnp.bfloat16)
    remote(items.at[core], items.at[core], it_send.at[0], it_recv.at[0], sibling).start()
    remote(shifts.at[core], shifts.at[core], it_send.at[1], it_recv.at[1], sibling).start()
    remote(items.at[other], items.at[other], it_send.at[0], it_recv.at[0], sibling).wait_recv()
    remote(shifts.at[other], shifts.at[other], it_send.at[1], it_recv.at[1], sibling).wait_recv()
    for side in range(2):
        items_t[:, pl.ds(side * half, half)] = items[side].T

    row_ids = lax.broadcasted_iota(jnp.int32, (half, rows), 0)
    base = col * (2 * half)

    def score_chunk(c):
        tops = []
        picks = []
        for side in range(2):
            product = lax.dot_general(
                items[side], q_all[c], (((1,), (1,)), ((), ())), preferred_element_type=jnp.float32
            )
            shift = shifts[side][:, None, :, :]
            value = (logit_scale * product).reshape(slots, BLOCK // 8, 8, rows) - shift
            value = value.reshape(half, rows)
            scores[c, side] = value
            marked = row_ids == t_all[c][0:1, :] - (base + side * half)
            tops.append(jnp.max(value, axis=0, keepdims=True))
            picks.append(jnp.sum(jnp.where(marked, value, 0.0), axis=0, keepdims=True))
        top = jnp.maximum(tops[0], tops[1])
        total = jnp.zeros((1, rows), jnp.float32)
        for side in range(2):
            total = total + jnp.sum(jnp.exp(scores[c, side] - top), axis=0, keepdims=True)
        stats[col, pl.ds(c, 1), :] = top
        stats[col, pl.ds(n_col + c, 1), :] = total
        pick_own[c] = jnp.broadcast_to(picks[0] + picks[1], (8, rows))

    load_own.wait()
    score_chunk(col)

    @pl.loop(1, n_col)
    def _(step):
        c = (col + step) % n_col
        remote(q_all.at[c], q_all.at[c], q_send.at[c], q_recv.at[c], sibling).wait_recv()
        remote(t_all.at[c], t_all.at[c], t_send.at[c], t_recv.at[c], sibling).wait_recv()
        score_chunk(c)

    for step in range(1, n_col):
        c = (col + step) % n_col
        remote(stats.at[col], stats.at[col], st_send.at[c], st_recv.at[col], column(c)).start()
    for step in range(1, n_col):
        c = (col + step) % n_col
        remote(pick_own.at[c], pick_all.at[col], pk_send.at[c], pk_recv.at[col], column(c)).start()
    for step in range(1, n_col):
        c = (col + step) % n_col
        remote(stats.at[c], stats.at[c], st_send.at[c], st_recv.at[c], sibling).wait_recv()

    top = stats[0, 0:n_col, :]
    for c in range(1, n_col):
        top = jnp.maximum(top, stats[c, 0:n_col, :])
    total = jnp.zeros_like(top)
    for c in range(n_col):
        total = total + stats[c, n_col : 2 * n_col, :] * jnp.exp(stats[c, 0:n_col, :] - top)
    norm[...] = top + jnp.log(total)

    every_query = q_all[...].reshape(n_col * rows, width)

    slot_rows = lax.broadcasted_iota(jnp.int32, (BLOCK, rows), 0)

    def item_part(side, j):
        @pl.loop(0, n_col)
        def _(c):
            marked = slot_rows == t_all[c][0:1, :] - (base + side * half + j * BLOCK)
            probs = jnp.exp(scores[c, side, pl.ds(j * BLOCK, BLOCK), :] - norm[pl.ds(c, 1), :])
            value = (probs - marked.astype(jnp.float32)).astype(jnp.bfloat16)
            dlog[side, pl.ds(j * BLOCK, BLOCK), pl.ds(pl.multiple_of(c * rows, rows), rows)] = value

        return logit_scale * jnp.dot(
            dlog[side, pl.ds(j * BLOCK, BLOCK), :], every_query, preferred_element_type=jnp.float32
        )

    def to_sibling(j):
        where = pl.ds(j * BLOCK, BLOCK)
        return remote(part_out.at[where, :], part_in.at[where, :], gp_send.at[j], gp_recv.at[j], sibling)

    for j in range(slots):
        part_out[pl.ds(j * BLOCK, BLOCK), :] = item_part(other, j).astype(jnp.bfloat16)
        to_sibling(j).start()
    for j in range(slots):
        part_own[pl.ds(j * BLOCK, BLOCK), :] = item_part(core, j)

    def query_part(c):
        lanes = pl.ds(pl.multiple_of(c * rows, rows), rows)
        value = jnp.dot(items_t[:, pl.ds(0, half)], dlog[0, :, lanes], preferred_element_type=jnp.float32)
        value += jnp.dot(items_t[:, pl.ds(half, half)], dlog[1, :, lanes], preferred_element_type=jnp.float32)
        return logit_scale * value

    @pl.loop(1, n_col)
    def _(step):
        c = (col + step) % n_col
        qg_out[c] = query_part(c).astype(jnp.bfloat16)
        remote(qg_out.at[c], qg_in.at[col], qg_send.at[c], qg_recv.at[col], column(c)).start()

    def exchange_slot(h, j):
        where = pl.ds(j * BLOCK, BLOCK)
        return remote(
            s_out.at[h, where, :], s_in.at[h, where, :], ss_send.at[h, j], ss_recv.at[h, j], flipped(h % bits)
        )

    for j in range(slots):
        where = pl.ds(j * BLOCK, BLOCK)
        to_sibling(j).wait_recv()
        value = part_own[where, :] + part_in[where, :].astype(jnp.float32)
        for h in range(2):
            s_out[h, where, :] = value[:, h * half_width : (h + 1) * half_width].astype(jnp.bfloat16)
            exchange_slot(h, j).start()

    def exchange(stage, h, g):
        where = pl.ds(g * group, group)
        return remote(
            bf_out.at[stage - 1, h, where, :], bf_in.at[stage - 1, h, where, :],
            bf_send.at[stage - 1, h, g], bf_recv.at[stage - 1, h, g], flipped((stage + h) % bits),
        )

    def pass_on(stage, h, g, value):
        if stage < bits:
            bf_out[stage - 1, h, pl.ds(g * group, group), :] = value.astype(jnp.bfloat16)
            exchange(stage, h, g).start()
        else:
            grad_ref[pl.ds(g * group, group), pl.ds(h * half_width, half_width)] = value

    qg_own[...] = query_part(col)
    for h in range(2):
        announce(h).wait_recv()
        for j in range(slots):
            exchange_slot(h, j).wait_recv()
    for g in range(groups):
        for h in range(2):
            pieces = []
            for b in range(g * group // BLOCK, (g + 1) * group // BLOCK):
                mine = jnp.zeros((BLOCK // 8, 8, half_width), jnp.float32)
                theirs = mine
                for j in range(slots):
                    where = pl.ds(j * BLOCK, BLOCK)
                    mine = mine + is_block(id_own[j], b) * tiles(s_out[h, where, :])
                    theirs = theirs + is_block(id_in[h, j], b) * tiles(s_in[h, where, :])
                pieces.append((mine + theirs).reshape(BLOCK, half_width))
            pass_on(1, h, g, jnp.concatenate(pieces, axis=0))

    total_qg = qg_own[...]
    picked = pick_own[col]
    for step in range(1, n_col):
        c = (col + step) % n_col
        remote(qg_in.at[c], qg_in.at[c], qg_send.at[c], qg_recv.at[c], sibling).wait_recv()
        remote(pick_all.at[c], pick_all.at[c], pk_send.at[c], pk_recv.at[c], sibling).wait_recv()
        total_qg = total_qg + qg_in[c].astype(jnp.float32)
        picked = picked + pick_all[c]
    qgrad_ref[0] = total_qg.T
    loss_ref[...] = norm[pl.ds(col, 1), :] - picked[0:1, :]

    for stage in range(1, bits):
        for g in range(groups):
            for h in range(2):
                where = pl.ds(g * group, group)
                exchange(stage, h, g).wait_recv()
                value = bf_out[stage - 1, h, where, :].astype(jnp.float32)
                value = value + bf_in[stage - 1, h, where, :].astype(jnp.float32)
                pass_on(stage + 1, h, g, value)

    for step in range(1, n_col):
        c = (col + step) % n_col
        remote(q_all.at[col], q_all.at[col], q_send.at[c], q_recv.at[c], sibling).wait_send()
        remote(t_all.at[col], t_all.at[col], t_send.at[c], t_recv.at[c], sibling).wait_send()
        remote(stats.at[col], stats.at[col], st_send.at[c], st_recv.at[c], sibling).wait_send()
        remote(pick_own.at[c], pick_own.at[c], pk_send.at[c], pk_recv.at[c], sibling).wait_send()
        remote(qg_out.at[c], qg_out.at[c], qg_send.at[c], qg_recv.at[c], sibling).wait_send()
    remote(items.at[core], items.at[core], it_send.at[0], it_recv.at[0], sibling).wait_send()
    remote(shifts.at[core], shifts.at[core], it_send.at[1], it_recv.at[1], sibling).wait_send()
    for j in range(slots):
        to_sibling(j).wait_send()
    for h in range(2):
        announce(h).wait_send()
        for j in range(slots):
            exchange_slot(h, j).wait_send()
        for stage in range(1, bits):
            for g in range(groups):
                exchange(stage, h, g).wait_send()


def local(n_rep, n_shard, queries, targets, samp_ids, counts, logq, table, first_moment, second_moment):
    rows, width = queries.shape[1:]
    slots = samp_ids.shape[1]
    items_held = table.shape[0]
    blocks = items_held // BLOCK
    n_col = n_shard // 2
    bits = n_rep.bit_length() - 1
    half = slots * BLOCK
    f32, bf16 = jnp.float32, jnp.bfloat16
    dma = pltpu.SemaphoreType.DMA
    vmem = pl.BlockSpec(memory_space=pltpu.VMEM)
    pair_flops = n_col * rows * 2 * half * width
    own_loss, query_grad, gradient = pl.pallas_call(
        functools.partial(kernel, n_rep, n_col, slots, blocks),
        out_shape=(
            jax.ShapeDtypeStruct((1, rows), f32),
            jax.ShapeDtypeStruct((1, rows, width), f32),
            jax.ShapeDtypeStruct((items_held, width), f32),
        ),
        in_specs=[pl.BlockSpec(memory_space=pltpu.HBM)] * 6,
        out_specs=(vmem, vmem, vmem),
        scratch_shapes=[
            pltpu.SMEM((1, slots), jnp.int32),
            pltpu.SMEM((1, 1), jnp.int32),
            pltpu.SMEM((1, slots), f32),
            pltpu.VMEM((1, rows), jnp.int32),
            pltpu.VMEM((items_held, width), f32),
            pltpu.VMEM((slots, 8, BLOCK), f32),
            pltpu.VMEM((2, slots, 8, BLOCK), f32),
            pltpu.VMEM((2, half, width // 2), bf16),
            pltpu.VMEM((2, half, width // 2), bf16),
            pltpu.VMEM((n_col, rows, width), bf16),
            pltpu.VMEM((n_col, 8, rows), jnp.int32),
            pltpu.VMEM((2, half, width), bf16),
            pltpu.VMEM((width, 2 * half), bf16),
            pltpu.VMEM((2, slots, 8, BLOCK), f32),
            pltpu.VMEM((n_col, 2, half, rows), f32),
            pltpu.VMEM((2, half, n_col * rows), bf16),
            pltpu.VMEM((n_col, 2 * n_col, rows), f32),
            pltpu.VMEM((n_col, rows), f32),
            pltpu.VMEM((n_col, 8, rows), f32),
            pltpu.VMEM((n_col, 8, rows), f32),
            pltpu.VMEM((half, width), f32),
            pltpu.VMEM((half, width), bf16),
            pltpu.VMEM((half, width), bf16),
            pltpu.VMEM((width, rows), f32),
            pltpu.VMEM((n_col, width, rows), bf16),
            pltpu.VMEM((n_col, width, rows), bf16),
            pltpu.VMEM((max(bits - 1, 1), 2, items_held, width // 2), bf16),
            pltpu.VMEM((max(bits - 1, 1), 2, items_held, width // 2), bf16),
            dma((4,)), dma(()), dma(()), dma((2,)), dma((2,)), dma((2, slots)), dma((2, slots)),
            dma((n_col,)), dma((n_col,)), dma((n_col,)), dma((n_col,)),
            dma((2,)), dma((2,)),
            dma((n_col,)), dma((n_col,)), dma((n_col,)), dma((n_col,)),
            dma((slots,)), dma((slots,)),
            dma((n_col,)), dma((n_col,)),
            dma((bits, 2, blocks)), dma((bits, 2, blocks)),
        ],
        compiler_params=pltpu.CompilerParams(
            collective_id=0, has_side_effects=True, vmem_limit_bytes=60 * 1024 * 1024
        ),
        cost_estimate=pl.CostEstimate(
            flops=6 * pair_flops, bytes_accessed=4 * items_held * width, transcendentals=2 * pair_flops // width
        ),
    )(samp_ids, counts, logq, targets, queries, table)
    new_table, new_first, new_second = adam_update(table, first_moment, second_moment, gradient)
    return (own_loss, query_grad, new_table, new_first, new_second)


def solution(mesh):
    in_specs = (
        P("rep", "shard", None),
        P("rep", "shard"),
        P("rep", "shard"),
        P("rep", "shard"),
        P("rep", "shard"),
        P("shard", None),
        P("shard", None),
        P("shard", None),
    )
    out_specs = (
        P("rep", "shard"),
        P("rep", "shard", None),
        P("shard", None),
        P("shard", None),
        P("shard", None),
    )
    step = functools.partial(local, mesh.shape["rep"], mesh.shape["shard"])
    return jax.shard_map(step, mesh=mesh, in_specs=in_specs, out_specs=out_specs, check_vma=False)
```

```python
import functools

import jax
import jax.numpy as jnp
from jax import lax
from jax.experimental import pallas as pl
from jax.experimental.pallas import tpu as pltpu
from jax.sharding import PartitionSpec as P

BLOCK = 128
MESH = pl.DeviceIdType.MESH

logit_scale = 2.0
beta_first = 0.9
beta_second = 0.99
learn_rate = 0.01
adam_eps = 1e-08
bias_first = 1.0 - 0.9**10
bias_second = 1.0 - 0.99**10
dead_shift = 1e30


def adam_update(weights, first, second, gradient):
    first = beta_first * first + (1.0 - beta_first) * gradient
    second = beta_second * second + (1.0 - beta_second) * gradient * gradient
    weights = weights - learn_rate * (first / bias_first) / (
        jnp.sqrt(second / bias_second) + adam_eps
    )
    return (weights, first, second)


def finish_kernel(
    loss_ref, qgrad_ref, grad_ref, table_ref, first_ref, second_ref,
    loss_out, qgrad_out, table_out, first_out, second_out,
):
    @pl.when(pl.program_id(0) == 0)
    def _():
        loss_out[...] = loss_ref[...]
        qgrad_out[...] = qgrad_ref[...]

    table_out[...], first_out[...], second_out[...] = adam_update(
        table_ref[...], first_ref[...], second_ref[...], grad_ref[...]
    )


def kernel(
    n_rep, n_col, slots, blocks,
    ids_hbm, counts_hbm, logq_hbm, targets_hbm, queries_ref, table_ref,
    loss_ref, qgrad_ref, grad_ref,
    ids_ref, counts_ref, logq_ref, targets_ref, table_v, id_own, id_in, s_out, s_in, q_all, t_all, items, items_t, shifts, scores, dlog, stats, norm, pick_own, pick_all,
    part_own, part_out, part_in, qg_own, qg_out, qg_in, bf_out, bf_in,
    small_sem, own_sem, table_sem, id_send, id_recv, ss_send, ss_recv, q_send, q_recv, t_send, t_recv, it_send, it_recv, st_send, st_recv, pk_send, pk_recv,
    gp_send, gp_recv, qg_send, qg_recv, bf_send, bf_recv,
):
    rep = lax.axis_index("rep")
    shard = lax.axis_index("shard")
    col = shard // 2
    core = shard % 2
    rows = queries_ref.shape[1]
    width = queries_ref.shape[2]
    half_width = width // 2
    half = slots * BLOCK
    bits = n_rep.bit_length() - 1
    group = BLOCK * (2 if blocks % 2 == 0 else 1)
    groups = blocks * BLOCK // group
    sibling = {"rep": rep, "shard": col * 2 + (1 - core)}
    other = 1 - core

    def column(c):
        return {"rep": rep, "shard": c * 2 + core}

    def flipped(bit):
        size = 1 << bit
        return {"rep": rep + size * (1 - 2 * ((rep // size) % 2)), "shard": shard}

    def remote(src, dst, send, recv, device):
        return pltpu.make_async_remote_copy(
            src_ref=src, dst_ref=dst, send_sem=send, recv_sem=recv, device_id=device, device_id_type=MESH
        )

    load_table = pltpu.make_async_copy(table_ref, table_v, table_sem)
    load_small = [
        pltpu.make_async_copy(src, dst, small_sem.at[i])
        for i, (src, dst) in enumerate(
            [(ids_hbm, ids_ref), (counts_hbm, counts_ref), (logq_hbm, logq_ref), (targets_hbm, targets_ref)]
        )
    ]
    load_own = pltpu.make_async_copy(queries_ref.at[0], q_all.at[col], own_sem)
    for load in load_small:
        load.start()
    load_own.start()
    load_table.start()

    barrier = pltpu.get_barrier_semaphore()
    for step in range(1, n_col):
        pl.semaphore_signal(barrier, inc=1, device_id=column((col + step) % n_col), device_id_type=MESH)
    pl.semaphore_signal(barrier, inc=1, device_id=sibling, device_id_type=MESH)
    for bit in range(bits):
        pl.semaphore_signal(barrier, inc=1, device_id=flipped(bit), device_id_type=MESH)
    for load in load_small:
        load.wait()
    t_all[col] = jnp.broadcast_to(targets_ref[...], (8, rows))
    count = counts_ref[0, 0]
    for j in range(slots):
        shift = jnp.where(j < count, logq_ref[0, j], dead_shift)
        shifts[core, j] = jnp.full((8, BLOCK), shift, jnp.float32)
        id_own[j] = jnp.full((8, BLOCK), ids_ref[0, j].astype(jnp.float32), jnp.float32)
    pl.semaphore_wait(barrier, n_col + bits)

    for step in range(1, n_col):
        c = (col + step) % n_col
        remote(queries_ref.at[0], q_all.at[col], q_send.at[c], q_recv.at[col], column(c)).start()
        remote(t_all.at[col], t_all.at[col], t_send.at[c], t_recv.at[col], column(c)).start()

    def announce(h):
        return remote(id_own, id_in.at[h], id_send.at[h], id_recv.at[h], flipped(h % bits))

    for h in range(2):
        announce(h).start()

    def is_block(tile, b):
        return jnp.where(tile == float(b), 1.0, 0.0)[None]

    def tiles(value):
        return value.astype(jnp.float32).reshape(BLOCK // 8, 8, half_width)

    load_table.wait()
    for j in range(slots):
        for h in range(2):
            value = jnp.zeros((BLOCK // 8, 8, half_width), jnp.float32)
            for b in range(blocks):
                held = table_v[pl.ds(b * BLOCK, BLOCK), pl.ds(h * half_width, half_width)]
                value = value + is_block(id_own[j], b) * tiles(held)
            items[core, pl.ds(j * BLOCK, BLOCK), pl.ds(h * half_width, half_width)] = value.reshape(
                BLOCK, half_width
            ).astype(jnp.bfloat16)
    remote(items.at[core], items.at[core], it_send.at[0], it_recv.at[0], sibling).start()
    remote(shifts.at[core], shifts.at[core], it_send.at[1], it_recv.at[1], sibling).start()
    remote(items.at[other], items.at[other], it_send.at[0], it_recv.at[0], sibling).wait_recv()
    remote(shifts.at[other], shifts.at[other], it_send.at[1], it_recv.at[1], sibling).wait_recv()
    for side in range(2):
        items_t[:, pl.ds(side * half, half)] = items[side].T

    row_ids = lax.broadcasted_iota(jnp.int32, (half, rows), 0)
    base = col * (2 * half)

    def score_chunk(c):
        tops = []
        picks = []
        for side in range(2):
            product = lax.dot_general(
                items[side], q_all[c], (((1,), (1,)), ((), ())), preferred_element_type=jnp.float32
            )
            shift = shifts[side][:, None, :, :]
            value = (logit_scale * product).reshape(slots, BLOCK // 8, 8, rows) - shift
            value = value.reshape(half, rows)
            scores[c, side] = value
            marked = row_ids == t_all[c][0:1, :] - (base + side * half)
            tops.append(jnp.max(value, axis=0, keepdims=True))
            picks.append(jnp.sum(jnp.where(marked, value, 0.0), axis=0, keepdims=True))
        top = jnp.maximum(tops[0], tops[1])
        total = jnp.zeros((1, rows), jnp.float32)
        for side in range(2):
            total = total + jnp.sum(jnp.exp(scores[c, side] - top), axis=0, keepdims=True)
        stats[col, pl.ds(c, 1), :] = top
        stats[col, pl.ds(n_col + c, 1), :] = total
        pick_own[c] = jnp.broadcast_to(picks[0] + picks[1], (8, rows))

    load_own.wait()
    score_chunk(col)

    @pl.loop(1, n_col)
    def _(step):
        c = (col + step) % n_col
        remote(q_all.at[c], q_all.at[c], q_send.at[c], q_recv.at[c], sibling).wait_recv()
        remote(t_all.at[c], t_all.at[c], t_send.at[c], t_recv.at[c], sibling).wait_recv()
        score_chunk(c)

    for step in range(1, n_col):
        c = (col + step) % n_col
        remote(stats.at[col], stats.at[col], st_send.at[c], st_recv.at[col], column(c)).start()
    for step in range(1, n_col):
        c = (col + step) % n_col
        remote(pick_own.at[c], pick_all.at[col], pk_send.at[c], pk_recv.at[col], column(c)).start()
    for step in range(1, n_col):
        c = (col + step) % n_col
        remote(stats.at[c], stats.at[c], st_send.at[c], st_recv.at[c], sibling).wait_recv()

    top = stats[0, 0:n_col, :]
    for c in range(1, n_col):
        top = jnp.maximum(top, stats[c, 0:n_col, :])
    total = jnp.zeros_like(top)
    for c in range(n_col):
        total = total + stats[c, n_col : 2 * n_col, :] * jnp.exp(stats[c, 0:n_col, :] - top)
    norm[...] = top + jnp.log(total)

    every_query = q_all[...].reshape(n_col * rows, width)

    slot_rows = lax.broadcasted_iota(jnp.int32, (BLOCK, rows), 0)

    def item_part(side, j):
        @pl.loop(0, n_col)
        def _(c):
            marked = slot_rows == t_all[c][0:1, :] - (base + side * half + j * BLOCK)
            probs = jnp.exp(scores[c, side, pl.ds(j * BLOCK, BLOCK), :] - norm[pl.ds(c, 1), :])
            value = (probs - marked.astype(jnp.float32)).astype(jnp.bfloat16)
            dlog[side, pl.ds(j * BLOCK, BLOCK), pl.ds(pl.multiple_of(c * rows, rows), rows)] = value

        return logit_scale * jnp.dot(
            dlog[side, pl.ds(j * BLOCK, BLOCK), :], every_query, preferred_element_type=jnp.float32
        )

    def to_sibling(j):
        where = pl.ds(j * BLOCK, BLOCK)
        return remote(part_out.at[where, :], part_in.at[where, :], gp_send.at[j], gp_recv.at[j], sibling)

    for j in range(slots):
        part_out[pl.ds(j * BLOCK, BLOCK), :] = item_part(other, j).astype(jnp.bfloat16)
        to_sibling(j).start()
    for j in range(slots):
        part_own[pl.ds(j * BLOCK, BLOCK), :] = item_part(core, j)

    def query_part(c):
        lanes = pl.ds(pl.multiple_of(c * rows, rows), rows)
        value = jnp.dot(items_t[:, pl.ds(0, half)], dlog[0, :, lanes], preferred_element_type=jnp.float32)
        value += jnp.dot(items_t[:, pl.ds(half, half)], dlog[1, :, lanes], preferred_element_type=jnp.float32)
        return logit_scale * value

    @pl.loop(1, n_col)
    def _(step):
        c = (col + step) % n_col
        qg_out[c] = query_part(c).astype(jnp.bfloat16)
        remote(qg_out.at[c], qg_in.at[col], qg_send.at[c], qg_recv.at[col], column(c)).start()

    def exchange_slot(h, j):
        where = pl.ds(j * BLOCK, BLOCK)
        return remote(
            s_out.at[h, where, :], s_in.at[h, where, :], ss_send.at[h, j], ss_recv.at[h, j], flipped(h % bits)
        )

    for j in range(slots):
        where = pl.ds(j * BLOCK, BLOCK)
        to_sibling(j).wait_recv()
        value = part_own[where, :] + part_in[where, :].astype(jnp.float32)
        for h in range(2):
            s_out[h, where, :] = value[:, h * half_width : (h + 1) * half_width].astype(jnp.bfloat16)
            exchange_slot(h, j).start()

    def exchange(stage, h, g):
        where = pl.ds(g * group, group)
        return remote(
            bf_out.at[stage - 1, h, where, :], bf_in.at[stage - 1, h, where, :],
            bf_send.at[stage - 1, h, g], bf_recv.at[stage - 1, h, g], flipped((stage + h) % bits),
        )

    def pass_on(stage, h, g, value):
        if stage < bits:
            bf_out[stage - 1, h, pl.ds(g * group, group), :] = value.astype(jnp.bfloat16)
            exchange(stage, h, g).start()
        else:
            grad_ref[pl.ds(g * group, group), pl.ds(h * half_width, half_width)] = value

    qg_own[...] = query_part(col)
    for h in range(2):
        announce(h).wait_recv()
        for j in range(slots):
            exchange_slot(h, j).wait_recv()
    for g in range(groups):
        for h in range(2):
            pieces = []
            for b in range(g * group // BLOCK, (g + 1) * group // BLOCK):
                mine = jnp.zeros((BLOCK // 8, 8, half_width), jnp.float32)
                theirs = mine
                for j in range(slots):
                    where = pl.ds(j * BLOCK, BLOCK)
                    mine = mine + is_block(id_own[j], b) * tiles(s_out[h, where, :])
                    theirs = theirs + is_block(id_in[h, j], b) * tiles(s_in[h, where, :])
                pieces.append((mine + theirs).reshape(BLOCK, half_width))
            pass_on(1, h, g, jnp.concatenate(pieces, axis=0))

    total_qg = qg_own[...]
    picked = pick_own[col]
    for step in range(1, n_col):
        c = (col + step) % n_col
        remote(qg_in.at[c], qg_in.at[c], qg_send.at[c], qg_recv.at[c], sibling).wait_recv()
        remote(pick_all.at[c], pick_all.at[c], pk_send.at[c], pk_recv.at[c], sibling).wait_recv()
        total_qg = total_qg + qg_in[c].astype(jnp.float32)
        picked = picked + pick_all[c]
    qgrad_ref[0] = total_qg.T
    loss_ref[...] = norm[pl.ds(col, 1), :] - picked[0:1, :]

    for stage in range(1, bits):
        for g in range(groups):
            for h in range(2):
                where = pl.ds(g * group, group)
                exchange(stage, h, g).wait_recv()
                value = bf_out[stage - 1, h, where, :].astype(jnp.float32)
                value = value + bf_in[stage - 1, h, where, :].astype(jnp.float32)
                pass_on(stage + 1, h, g, value)

    for step in range(1, n_col):
        c = (col + step) % n_col
        remote(q_all.at[col], q_all.at[col], q_send.at[c], q_recv.at[c], sibling).wait_send()
        remote(t_all.at[col], t_all.at[col], t_send.at[c], t_recv.at[c], sibling).wait_send()
        remote(stats.at[col], stats.at[col], st_send.at[c], st_recv.at[c], sibling).wait_send()
        remote(pick_own.at[c], pick_own.at[c], pk_send.at[c], pk_recv.at[c], sibling).wait_send()
        remote(qg_out.at[c], qg_out.at[c], qg_send.at[c], qg_recv.at[c], sibling).wait_send()
    remote(items.at[core], items.at[core], it_send.at[0], it_recv.at[0], sibling).wait_send()
    remote(shifts.at[core], shifts.at[core], it_send.at[1], it_recv.at[1], sibling).wait_send()
    for j in range(slots):
        to_sibling(j).wait_send()
    for h in range(2):
        announce(h).wait_send()
        for j in range(slots):
            exchange_slot(h, j).wait_send()
        for stage in range(1, bits):
            for g in range(groups):
                exchange(stage, h, g).wait_send()


def local(n_rep, n_shard, queries, targets, samp_ids, counts, logq, table, first_moment, second_moment):
    rows, width = queries.shape[1:]
    slots = samp_ids.shape[1]
    items_held = table.shape[0]
    blocks = items_held // BLOCK
    n_col = n_shard // 2
    bits = n_rep.bit_length() - 1
    half = slots * BLOCK
    f32, bf16 = jnp.float32, jnp.bfloat16
    dma = pltpu.SemaphoreType.DMA
    vmem = pl.BlockSpec(memory_space=pltpu.VMEM)
    pair_flops = n_col * rows * 2 * half * width
    own_loss, query_grad, gradient = pl.pallas_call(
        functools.partial(kernel, n_rep, n_col, slots, blocks),
        out_shape=(
            jax.ShapeDtypeStruct((1, rows), f32),
            jax.ShapeDtypeStruct((1, rows, width), f32),
            jax.ShapeDtypeStruct((items_held, width), f32),
        ),
        in_specs=[pl.BlockSpec(memory_space=pltpu.HBM)] * 6,
        out_specs=(vmem, vmem, vmem),
        scratch_shapes=[
            pltpu.SMEM((1, slots), jnp.int32),
            pltpu.SMEM((1, 1), jnp.int32),
            pltpu.SMEM((1, slots), f32),
            pltpu.VMEM((1, rows), jnp.int32),
            pltpu.VMEM((items_held, width), f32),
            pltpu.VMEM((slots, 8, BLOCK), f32),
            pltpu.VMEM((2, slots, 8, BLOCK), f32),
            pltpu.VMEM((2, half, width // 2), bf16),
            pltpu.VMEM((2, half, width // 2), bf16),
            pltpu.VMEM((n_col, rows, width), bf16),
            pltpu.VMEM((n_col, 8, rows), jnp.int32),
            pltpu.VMEM((2, half, width), bf16),
            pltpu.VMEM((width, 2 * half), bf16),
            pltpu.VMEM((2, slots, 8, BLOCK), f32),
            pltpu.VMEM((n_col, 2, half, rows), f32),
            pltpu.VMEM((2, half, n_col * rows), bf16),
            pltpu.VMEM((n_col, 2 * n_col, rows), f32),
            pltpu.VMEM((n_col, rows), f32),
            pltpu.VMEM((n_col, 8, rows), f32),
            pltpu.VMEM((n_col, 8, rows), f32),
            pltpu.VMEM((half, width), f32),
            pltpu.VMEM((half, width), bf16),
            pltpu.VMEM((half, width), bf16),
            pltpu.VMEM((width, rows), f32),
            pltpu.VMEM((n_col, width, rows), bf16),
            pltpu.VMEM((n_col, width, rows), bf16),
            pltpu.VMEM((max(bits - 1, 1), 2, items_held, width // 2), bf16),
            pltpu.VMEM((max(bits - 1, 1), 2, items_held, width // 2), bf16),
            dma((4,)), dma(()), dma(()), dma((2,)), dma((2,)), dma((2, slots)), dma((2, slots)),
            dma((n_col,)), dma((n_col,)), dma((n_col,)), dma((n_col,)),
            dma((2,)), dma((2,)),
            dma((n_col,)), dma((n_col,)), dma((n_col,)), dma((n_col,)),
            dma((slots,)), dma((slots,)),
            dma((n_col,)), dma((n_col,)),
            dma((bits, 2, blocks)), dma((bits, 2, blocks)),
        ],
        compiler_params=pltpu.CompilerParams(
            collective_id=0, has_side_effects=True, vmem_limit_bytes=60 * 1024 * 1024
        ),
        cost_estimate=pl.CostEstimate(
            flops=6 * pair_flops, bytes_accessed=4 * items_held * width, transcendentals=2 * pair_flops // width
        ),
    )(samp_ids, counts, logq, targets, queries, table)
    tile = BLOCK * (2 if blocks % 2 == 0 else 1)
    by_tile = pl.BlockSpec((tile, width), lambda i: (i, 0))
    loss_spec = pl.BlockSpec((1, rows), lambda i: (0, 0))
    qgrad_spec = pl.BlockSpec((1, rows, width), lambda i: (0, 0, 0))
    held = jax.ShapeDtypeStruct((items_held, width), f32)
    return pl.pallas_call(
        finish_kernel,
        grid=(items_held // tile,),
        out_shape=(
            jax.ShapeDtypeStruct((1, rows), f32),
            jax.ShapeDtypeStruct((1, rows, width), f32),
            held, held, held,
        ),
        in_specs=[loss_spec, qgrad_spec, by_tile, by_tile, by_tile, by_tile],
        out_specs=(loss_spec, qgrad_spec, by_tile, by_tile, by_tile),
        compiler_params=pltpu.CompilerParams(vmem_limit_bytes=60 * 1024 * 1024),
    )(own_loss, query_grad, gradient, table, first_moment, second_moment)


def solution(mesh):
    in_specs = (
        P("rep", "shard", None),
        P("rep", "shard"),
        P("rep", "shard"),
        P("rep", "shard"),
        P("rep", "shard"),
        P("shard", None),
        P("shard", None),
        P("shard", None),
    )
    out_specs = (
        P("rep", "shard"),
        P("rep", "shard", None),
        P("shard", None),
        P("shard", None),
        P("shard", None),
    )
    step = functools.partial(local, mesh.shape["rep"], mesh.shape["shard"])
    return jax.shard_map(step, mesh=mesh, in_specs=in_specs, out_specs=out_specs, check_vma=False)
```

```python
import functools

import jax
import jax.numpy as jnp
from jax import lax
from jax.experimental import pallas as pl
from jax.experimental.pallas import tpu as pltpu
from jax.sharding import PartitionSpec as P

BLOCK = 128
MESH = pl.DeviceIdType.MESH

logit_scale = 2.0
beta_first = 0.9
beta_second = 0.99
learn_rate = 0.01
adam_eps = 1e-08
bias_first = 1.0 - 0.9**10
bias_second = 1.0 - 0.99**10
dead_shift = 1e30


def adam_update(weights, first, second, gradient):
    first = beta_first * first + (1.0 - beta_first) * gradient
    second = beta_second * second + (1.0 - beta_second) * gradient * gradient
    weights = weights - learn_rate * (first / bias_first) / (
        jnp.sqrt(second / bias_second) + adam_eps
    )
    return (weights, first, second)


def finish_kernel(
    loss_ref, qgrad_ref, grad_ref, table_ref, first_ref, second_ref,
    loss_out, qgrad_out, table_out, first_out, second_out,
):
    @pl.when(pl.program_id(0) == 0)
    def _():
        loss_out[...] = loss_ref[...]
        qgrad_out[...] = qgrad_ref[...]

    table_out[...], first_out[...], second_out[...] = adam_update(
        table_ref[...], first_ref[...], second_ref[...], grad_ref[...]
    )


def kernel(
    n_rep, n_col, slots, blocks,
    ids_hbm, counts_hbm, logq_hbm, targets_hbm, queries_ref, table_ref,
    loss_ref, qgrad_ref, grad_ref,
    ids_ref, counts_ref, logq_ref, targets_ref, table_v, id_own, id_in, s_out, s_in, q_all, t_all, items, items_t, shifts, scores, dlog, stats, norm, pick_own, pick_all,
    part_own, part_out, part_in, qg_own, qg_out, qg_in, bf_out, bf_in,
    small_sem, own_sem, table_sem, id_send, id_recv, ss_send, ss_recv, q_send, q_recv, t_send, t_recv, it_send, it_recv, st_send, st_recv, pk_send, pk_recv,
    gp_send, gp_recv, qg_send, qg_recv, bf_send, bf_recv,
):
    rep = lax.axis_index("rep")
    shard = lax.axis_index("shard")
    col = shard // 2
    core = shard % 2
    rows = queries_ref.shape[1]
    width = queries_ref.shape[2]
    half_width = width // 2
    half = slots * BLOCK
    bits = n_rep.bit_length() - 1
    group = BLOCK * (2 if blocks % 2 == 0 else 1)
    groups = blocks * BLOCK // group
    sibling = {"rep": rep, "shard": col * 2 + (1 - core)}
    other = 1 - core

    def column(c):
        return {"rep": rep, "shard": c * 2 + core}

    def flipped(bit):
        size = 1 << bit
        return {"rep": rep + size * (1 - 2 * ((rep // size) % 2)), "shard": shard}

    def remote(src, dst, send, recv, device):
        return pltpu.make_async_remote_copy(
            src_ref=src, dst_ref=dst, send_sem=send, recv_sem=recv, device_id=device, device_id_type=MESH
        )

    load_table = pltpu.make_async_copy(table_ref, table_v, table_sem)
    load_small = [
        pltpu.make_async_copy(src, dst, small_sem.at[i])
        for i, (src, dst) in enumerate(
            [(ids_hbm, ids_ref), (counts_hbm, counts_ref), (logq_hbm, logq_ref), (targets_hbm, targets_ref)]
        )
    ]
    load_own = pltpu.make_async_copy(queries_ref.at[0], q_all.at[col], own_sem)
    for load in load_small:
        load.start()
    load_own.start()
    load_table.start()

    barrier = pltpu.get_barrier_semaphore()
    for step in range(1, n_col):
        pl.semaphore_signal(barrier, inc=1, device_id=column((col + step) % n_col), device_id_type=MESH)
    pl.semaphore_signal(barrier, inc=1, device_id=sibling, device_id_type=MESH)
    for bit in range(bits):
        pl.semaphore_signal(barrier, inc=1, device_id=flipped(bit), device_id_type=MESH)
    for load in load_small:
        load.wait()
    t_all[col] = jnp.broadcast_to(targets_ref[...], (8, rows))
    count = counts_ref[0, 0]
    for j in range(slots):
        shift = jnp.where(j < count, logq_ref[0, j], dead_shift)
        shifts[core, j] = jnp.full((8, BLOCK), shift, jnp.float32)
        id_own[j] = jnp.full((8, BLOCK), ids_ref[0, j].astype(jnp.float32), jnp.float32)
    pl.semaphore_wait(barrier, n_col + bits)

    for step in range(1, n_col):
        c = (col + step) % n_col
        remote(queries_ref.at[0], q_all.at[col], q_send.at[c], q_recv.at[col], column(c)).start()
        remote(t_all.at[col], t_all.at[col], t_send.at[c], t_recv.at[col], column(c)).start()

    def announce(h):
        return remote(id_own, id_in.at[h], id_send.at[h], id_recv.at[h], flipped(h % bits))

    for h in range(2):
        announce(h).start()

    def is_block(tile, b):
        return jnp.where(tile == float(b), 1.0, 0.0)[None]

    def tiles(value):
        return value.astype(jnp.float32).reshape(BLOCK // 8, 8, half_width)

    load_table.wait()
    for j in range(slots):
        for h in range(2):
            value = jnp.zeros((BLOCK // 8, 8, half_width), jnp.float32)
            for b in range(blocks):
                held = table_v[pl.ds(b * BLOCK, BLOCK), pl.ds(h * half_width, half_width)]
                value = value + is_block(id_own[j], b) * tiles(held)
            items[core, pl.ds(j * BLOCK, BLOCK), pl.ds(h * half_width, half_width)] = value.reshape(
                BLOCK, half_width
            ).astype(jnp.bfloat16)
    remote(items.at[core], items.at[core], it_send.at[0], it_recv.at[0], sibling).start()
    remote(shifts.at[core], shifts.at[core], it_send.at[1], it_recv.at[1], sibling).start()
    remote(items.at[other], items.at[other], it_send.at[0], it_recv.at[0], sibling).wait_recv()
    remote(shifts.at[other], shifts.at[other], it_send.at[1], it_recv.at[1], sibling).wait_recv()
    for side in range(2):
        items_t[:, pl.ds(side * half, half)] = items[side].T

    row_ids = lax.broadcasted_iota(jnp.int32, (half, rows), 0)
    base = col * (2 * half)

    def score_chunk(c):
        tops = []
        picks = []
        for side in range(2):
            product = lax.dot_general(
                items[side], q_all[c], (((1,), (1,)), ((), ())), preferred_element_type=jnp.float32
            )
            shift = shifts[side][:, None, :, :]
            value = (logit_scale * product).reshape(slots, BLOCK // 8, 8, rows) - shift
            value = value.reshape(half, rows)
            scores[c, side] = value
            marked = row_ids == t_all[c][0:1, :] - (base + side * half)
            tops.append(jnp.max(value, axis=0, keepdims=True))
            picks.append(jnp.sum(jnp.where(marked, value, 0.0), axis=0, keepdims=True))
        top = jnp.maximum(tops[0], tops[1])
        total = jnp.zeros((1, rows), jnp.float32)
        for side in range(2):
            total = total + jnp.sum(jnp.exp(scores[c, side] - top), axis=0, keepdims=True)
        stats[col, pl.ds(c, 1), :] = top
        stats[col, pl.ds(n_col + c, 1), :] = total
        pick_own[c] = jnp.broadcast_to(picks[0] + picks[1], (8, rows))

    load_own.wait()
    score_chunk(col)

    @pl.loop(1, n_col)
    def _(step):
        c = (col + step) % n_col
        remote(q_all.at[c], q_all.at[c], q_send.at[c], q_recv.at[c], sibling).wait_recv()
        remote(t_all.at[c], t_all.at[c], t_send.at[c], t_recv.at[c], sibling).wait_recv()
        score_chunk(c)

    for step in range(1, n_col):
        c = (col + step) % n_col
        remote(stats.at[col], stats.at[col], st_send.at[c], st_recv.at[col], column(c)).start()
    for step in range(1, n_col):
        c = (col + step) % n_col
        remote(pick_own.at[c], pick_all.at[col], pk_send.at[c], pk_recv.at[col], column(c)).start()
    for step in range(1, n_col):
        c = (col + step) % n_col
        remote(stats.at[c], stats.at[c], st_send.at[c], st_recv.at[c], sibling).wait_recv()

    top = stats[0, 0:n_col, :]
    for c in range(1, n_col):
        top = jnp.maximum(top, stats[c, 0:n_col, :])
    total = jnp.zeros_like(top)
    for c in range(n_col):
        total = total + stats[c, n_col : 2 * n_col, :] * jnp.exp(stats[c, 0:n_col, :] - top)
    norm[...] = top + jnp.log(total)

    every_query = q_all[...].reshape(n_col * rows, width)

    slot_rows = lax.broadcasted_iota(jnp.int32, (BLOCK, rows), 0)

    def item_part(side, j):
        @pl.loop(0, n_col)
        def _(c):
            marked = slot_rows == t_all[c][0:1, :] - (base + side * half + j * BLOCK)
            probs = jnp.exp(scores[c, side, pl.ds(j * BLOCK, BLOCK), :] - norm[pl.ds(c, 1), :])
            value = (probs - marked.astype(jnp.float32)).astype(jnp.bfloat16)
            dlog[side, pl.ds(j * BLOCK, BLOCK), pl.ds(pl.multiple_of(c * rows, rows), rows)] = value

        return logit_scale * jnp.dot(
            dlog[side, pl.ds(j * BLOCK, BLOCK), :], every_query, preferred_element_type=jnp.float32
        )

    def to_sibling(j):
        where = pl.ds(j * BLOCK, BLOCK)
        return remote(part_out.at[where, :], part_in.at[where, :], gp_send.at[j], gp_recv.at[j], sibling)

    for j in range(slots):
        part_out[pl.ds(j * BLOCK, BLOCK), :] = item_part(other, j).astype(jnp.bfloat16)
        to_sibling(j).start()
    for j in range(slots):
        part_own[pl.ds(j * BLOCK, BLOCK), :] = item_part(core, j)

    def query_part(c):
        lanes = pl.ds(pl.multiple_of(c * rows, rows), rows)
        value = jnp.dot(items_t[:, pl.ds(0, half)], dlog[0, :, lanes], preferred_element_type=jnp.float32)
        value += jnp.dot(items_t[:, pl.ds(half, half)], dlog[1, :, lanes], preferred_element_type=jnp.float32)
        return logit_scale * value

    @pl.loop(1, n_col)
    def _(step):
        c = (col + step) % n_col
        qg_out[c] = query_part(c).astype(jnp.bfloat16)
        remote(qg_out.at[c], qg_in.at[col], qg_send.at[c], qg_recv.at[col], column(c)).start()

    def exchange_slot(h, j):
        where = pl.ds(j * BLOCK, BLOCK)
        return remote(
            s_out.at[h, where, :], s_in.at[h, where, :], ss_send.at[h, j], ss_recv.at[h, j], flipped(h % bits)
        )

    for j in range(slots):
        where = pl.ds(j * BLOCK, BLOCK)
        to_sibling(j).wait_recv()
        value = part_own[where, :] + part_in[where, :].astype(jnp.float32)
        for h in range(2):
            s_out[h, where, :] = value[:, h * half_width : (h + 1) * half_width].astype(jnp.bfloat16)
            exchange_slot(h, j).start()

    def exchange(stage, h, g):
        where = pl.ds(g * group, group)
        return remote(
            bf_out.at[stage - 1, h, where, :], bf_in.at[stage - 1, h, where, :],
            bf_send.at[stage - 1, h, g], bf_recv.at[stage - 1, h, g], flipped((stage + h) % bits),
        )

    def pass_on(stage, h, g, value):
        if stage < bits:
            bf_out[stage - 1, h, pl.ds(g * group, group), :] = value.astype(jnp.bfloat16)
            exchange(stage, h, g).start()
        else:
            grad_ref[pl.ds(g * group, group), pl.ds(h * half_width, half_width)] = value

    qg_own[...] = query_part(col)
    for h in range(2):
        announce(h).wait_recv()
        for j in range(slots):
            exchange_slot(h, j).wait_recv()
    for g in range(groups):
        for h in range(2):
            pieces = []
            for b in range(g * group // BLOCK, (g + 1) * group // BLOCK):
                mine = jnp.zeros((BLOCK // 8, 8, half_width), jnp.float32)
                theirs = mine
                for j in range(slots):
                    where = pl.ds(j * BLOCK, BLOCK)
                    mine = mine + is_block(id_own[j], b) * tiles(s_out[h, where, :])
                    theirs = theirs + is_block(id_in[h, j], b) * tiles(s_in[h, where, :])
                pieces.append((mine + theirs).reshape(BLOCK, half_width))
            pass_on(1, h, g, jnp.concatenate(pieces, axis=0))

    total_qg = qg_own[...]
    picked = pick_own[col]
    for step in range(1, n_col):
        c = (col + step) % n_col
        remote(qg_in.at[c], qg_in.at[c], qg_send.at[c], qg_recv.at[c], sibling).wait_recv()
        remote(pick_all.at[c], pick_all.at[c], pk_send.at[c], pk_recv.at[c], sibling).wait_recv()
        total_qg = total_qg + qg_in[c].astype(jnp.float32)
        picked = picked + pick_all[c]
    qgrad_ref[0] = total_qg.T
    loss_ref[...] = norm[pl.ds(col, 1), :] - picked[0:1, :]

    for stage in range(1, bits):
        for g in range(groups):
            for h in range(2):
                where = pl.ds(g * group, group)
                exchange(stage, h, g).wait_recv()
                value = bf_out[stage - 1, h, where, :].astype(jnp.float32)
                value = value + bf_in[stage - 1, h, where, :].astype(jnp.float32)
                pass_on(stage + 1, h, g, value)

    for step in range(1, n_col):
        c = (col + step) % n_col
        remote(q_all.at[col], q_all.at[col], q_send.at[c], q_recv.at[c], sibling).wait_send()
        remote(t_all.at[col], t_all.at[col], t_send.at[c], t_recv.at[c], sibling).wait_send()
        remote(stats.at[col], stats.at[col], st_send.at[c], st_recv.at[c], sibling).wait_send()
        remote(pick_own.at[c], pick_own.at[c], pk_send.at[c], pk_recv.at[c], sibling).wait_send()
        remote(qg_out.at[c], qg_out.at[c], qg_send.at[c], qg_recv.at[c], sibling).wait_send()
    remote(items.at[core], items.at[core], it_send.at[0], it_recv.at[0], sibling).wait_send()
    remote(shifts.at[core], shifts.at[core], it_send.at[1], it_recv.at[1], sibling).wait_send()
    for j in range(slots):
        to_sibling(j).wait_send()
    for h in range(2):
        announce(h).wait_send()
        for j in range(slots):
            exchange_slot(h, j).wait_send()
        for stage in range(1, bits):
            for g in range(groups):
                exchange(stage, h, g).wait_send()


def local(n_rep, n_shard, queries, targets, samp_ids, counts, logq, table, first_moment, second_moment):
    rows, width = queries.shape[1:]
    slots = samp_ids.shape[1]
    items_held = table.shape[0]
    blocks = items_held // BLOCK
    n_col = n_shard // 2
    bits = n_rep.bit_length() - 1
    half = slots * BLOCK
    f32, bf16 = jnp.float32, jnp.bfloat16
    dma = pltpu.SemaphoreType.DMA
    vmem = pl.BlockSpec(memory_space=pltpu.VMEM)
    pair_flops = n_col * rows * 2 * half * width
    own_loss, query_grad, gradient = pl.pallas_call(
        functools.partial(kernel, n_rep, n_col, slots, blocks),
        out_shape=(
            jax.ShapeDtypeStruct((1, rows), f32),
            jax.ShapeDtypeStruct((1, rows, width), f32),
            jax.ShapeDtypeStruct((items_held, width), f32),
        ),
        in_specs=[pl.BlockSpec(memory_space=pltpu.HBM)] * 6,
        out_specs=(vmem, vmem, vmem),
        scratch_shapes=[
            pltpu.SMEM((1, slots), jnp.int32),
            pltpu.SMEM((1, 1), jnp.int32),
            pltpu.SMEM((1, slots), f32),
            pltpu.VMEM((1, rows), jnp.int32),
            pltpu.VMEM((items_held, width), f32),
            pltpu.VMEM((slots, 8, BLOCK), f32),
            pltpu.VMEM((2, slots, 8, BLOCK), f32),
            pltpu.VMEM((2, half, width // 2), bf16),
            pltpu.VMEM((2, half, width // 2), bf16),
            pltpu.VMEM((n_col, rows, width), bf16),
            pltpu.VMEM((n_col, 8, rows), jnp.int32),
            pltpu.VMEM((2, half, width), bf16),
            pltpu.VMEM((width, 2 * half), bf16),
            pltpu.VMEM((2, slots, 8, BLOCK), f32),
            pltpu.VMEM((n_col, 2, half, rows), f32),
            pltpu.VMEM((2, half, n_col * rows), bf16),
            pltpu.VMEM((n_col, 2 * n_col, rows), f32),
            pltpu.VMEM((n_col, rows), f32),
            pltpu.VMEM((n_col, 8, rows), f32),
            pltpu.VMEM((n_col, 8, rows), f32),
            pltpu.VMEM((half, width), f32),
            pltpu.VMEM((half, width), bf16),
            pltpu.VMEM((half, width), bf16),
            pltpu.VMEM((width, rows), f32),
            pltpu.VMEM((n_col, width, rows), bf16),
            pltpu.VMEM((n_col, width, rows), bf16),
            pltpu.VMEM((max(bits - 1, 1), 2, items_held, width // 2), bf16),
            pltpu.VMEM((max(bits - 1, 1), 2, items_held, width // 2), bf16),
            dma((4,)), dma(()), dma(()), dma((2,)), dma((2,)), dma((2, slots)), dma((2, slots)),
            dma((n_col,)), dma((n_col,)), dma((n_col,)), dma((n_col,)),
            dma((2,)), dma((2,)),
            dma((n_col,)), dma((n_col,)), dma((n_col,)), dma((n_col,)),
            dma((slots,)), dma((slots,)),
            dma((n_col,)), dma((n_col,)),
            dma((bits, 2, blocks)), dma((bits, 2, blocks)),
        ],
        compiler_params=pltpu.CompilerParams(
            collective_id=0, has_side_effects=True, vmem_limit_bytes=60 * 1024 * 1024
        ),
        cost_estimate=pl.CostEstimate(
            flops=6 * pair_flops, bytes_accessed=4 * items_held * width, transcendentals=2 * pair_flops // width
        ),
    )(samp_ids, counts, logq, targets, queries, table)
    tile = BLOCK
    by_tile = pl.BlockSpec((tile, width), lambda i: (i, 0))
    loss_spec = pl.BlockSpec((1, rows), lambda i: (0, 0))
    qgrad_spec = pl.BlockSpec((1, rows, width), lambda i: (0, 0, 0))
    held = jax.ShapeDtypeStruct((items_held, width), f32)
    return pl.pallas_call(
        finish_kernel,
        grid=(items_held // tile,),
        out_shape=(
            jax.ShapeDtypeStruct((1, rows), f32),
            jax.ShapeDtypeStruct((1, rows, width), f32),
            held, held, held,
        ),
        in_specs=[loss_spec, qgrad_spec, by_tile, by_tile, by_tile, by_tile],
        out_specs=(loss_spec, qgrad_spec, by_tile, by_tile, by_tile),
        compiler_params=pltpu.CompilerParams(vmem_limit_bytes=60 * 1024 * 1024),
    )(own_loss, query_grad, gradient, table, first_moment, second_moment)


def solution(mesh):
    in_specs = (
        P("rep", "shard", None),
        P("rep", "shard"),
        P("rep", "shard"),
        P("rep", "shard"),
        P("rep", "shard"),
        P("shard", None),
        P("shard", None),
        P("shard", None),
    )
    out_specs = (
        P("rep", "shard"),
        P("rep", "shard", None),
        P("shard", None),
        P("shard", None),
        P("shard", None),
    )
    step = functools.partial(local, mesh.shape["rep"], mesh.shape["shard"])
    return jax.shard_map(step, mesh=mesh, in_specs=in_specs, out_specs=out_specs, check_vma=False)
```

```python
import functools

import jax
import jax.numpy as jnp
from jax import lax
from jax.experimental import pallas as pl
from jax.experimental.pallas import tpu as pltpu
from jax.sharding import PartitionSpec as P

BLOCK = 128
MESH = pl.DeviceIdType.MESH

logit_scale = 2.0
beta_first = 0.9
beta_second = 0.99
learn_rate = 0.01
adam_eps = 1e-08
bias_first = 1.0 - 0.9**10
bias_second = 1.0 - 0.99**10
dead_shift = 1e30


def adam_update(weights, first, second, gradient):
    first = beta_first * first + (1.0 - beta_first) * gradient
    second = beta_second * second + (1.0 - beta_second) * gradient * gradient
    weights = weights - learn_rate * (first / bias_first) / (
        jnp.sqrt(second / bias_second) + adam_eps
    )
    return (weights, first, second)


def finish_kernel(
    loss_ref, qgrad_ref, grad_ref, table_ref, first_ref, second_ref,
    loss_out, qgrad_out, table_out, first_out, second_out,
):
    @pl.when(pl.program_id(0) == 0)
    def _():
        loss_out[...] = loss_ref[...]
        qgrad_out[...] = qgrad_ref[...]

    table_out[...], first_out[...], second_out[...] = adam_update(
        table_ref[...], first_ref[...], second_ref[...], grad_ref[...]
    )


def kernel(
    n_rep, n_col, slots, blocks,
    ids_hbm, counts_hbm, logq_hbm, targets_hbm, queries_ref, table_ref,
    loss_ref, qgrad_ref, grad_ref,
    ids_ref, counts_ref, logq_ref, targets_ref, table_v, id_own, id_in, s_out, s_in, q_all, t_all, items, items_t, shifts, scores, dlog, stats, norm, pick_own, pick_all,
    part_own, part_out, part_in, qg_own, qg_out, qg_in, bf_out, bf_in,
    small_sem, own_sem, table_sem, id_send, id_recv, ss_send, ss_recv, q_send, q_recv, t_send, t_recv, it_send, it_recv, st_send, st_recv, pk_send, pk_recv,
    gp_send, gp_recv, qg_send, qg_recv, bf_send, bf_recv,
):
    rep = lax.axis_index("rep")
    shard = lax.axis_index("shard")
    col = shard // 2
    core = shard % 2
    rows = queries_ref.shape[1]
    width = queries_ref.shape[2]
    half_width = width // 2
    half = slots * BLOCK
    bits = n_rep.bit_length() - 1
    group = BLOCK * (2 if blocks % 2 == 0 else 1)
    groups = blocks * BLOCK // group
    sibling = {"rep": rep, "shard": col * 2 + (1 - core)}
    other = 1 - core

    def column(c):
        return {"rep": rep, "shard": c * 2 + core}

    def flipped(bit):
        size = 1 << bit
        return {"rep": rep + size * (1 - 2 * ((rep // size) % 2)), "shard": shard}

    def remote(src, dst, send, recv, device):
        return pltpu.make_async_remote_copy(
            src_ref=src, dst_ref=dst, send_sem=send, recv_sem=recv, device_id=device, device_id_type=MESH
        )

    load_table = pltpu.make_async_copy(table_ref, table_v, table_sem)
    load_small = [
        pltpu.make_async_copy(src, dst, small_sem.at[i])
        for i, (src, dst) in enumerate(
            [(ids_hbm, ids_ref), (counts_hbm, counts_ref), (logq_hbm, logq_ref), (targets_hbm, targets_ref)]
        )
    ]
    load_own = pltpu.make_async_copy(queries_ref.at[0], q_all.at[col], own_sem)
    for load in load_small:
        load.start()
    load_own.start()
    load_table.start()

    barrier = pltpu.get_barrier_semaphore()
    for step in range(1, n_col):
        pl.semaphore_signal(barrier, inc=1, device_id=column((col + step) % n_col), device_id_type=MESH)
    pl.semaphore_signal(barrier, inc=1, device_id=sibling, device_id_type=MESH)
    for bit in range(bits):
        pl.semaphore_signal(barrier, inc=1, device_id=flipped(bit), device_id_type=MESH)
    for load in load_small:
        load.wait()
    t_all[col] = jnp.broadcast_to(targets_ref[...], (8, rows))
    count = counts_ref[0, 0]
    for j in range(slots):
        shift = jnp.where(j < count, logq_ref[0, j], dead_shift)
        shifts[core, j] = jnp.full((8, BLOCK), shift, jnp.float32)
        id_own[j] = jnp.full((8, BLOCK), ids_ref[0, j].astype(jnp.float32), jnp.float32)
    pl.semaphore_wait(barrier, n_col + bits)

    for step in range(1, n_col):
        c = (col + step) % n_col
        remote(queries_ref.at[0], q_all.at[col], q_send.at[c], q_recv.at[col], column(c)).start()
        remote(t_all.at[col], t_all.at[col], t_send.at[c], t_recv.at[col], column(c)).start()

    def announce(h):
        return remote(id_own, id_in.at[h], id_send.at[h], id_recv.at[h], flipped(h % bits))

    for h in range(2):
        announce(h).start()

    def is_block(tile, b):
        return jnp.where(tile == float(b), 1.0, 0.0)[None]

    def tiles(value):
        return value.astype(jnp.float32).reshape(BLOCK // 8, 8, half_width)

    load_table.wait()
    for j in range(slots):
        for h in range(2):
            value = jnp.zeros((BLOCK // 8, 8, half_width), jnp.float32)
            for b in range(blocks):
                held = table_v[pl.ds(b * BLOCK, BLOCK), pl.ds(h * half_width, half_width)]
                value = value + is_block(id_own[j], b) * tiles(held)
            items[core, pl.ds(j * BLOCK, BLOCK), pl.ds(h * half_width, half_width)] = value.reshape(
                BLOCK, half_width
            ).astype(jnp.bfloat16)
    remote(items.at[core], items.at[core], it_send.at[0], it_recv.at[0], sibling).start()
    remote(shifts.at[core], shifts.at[core], it_send.at[1], it_recv.at[1], sibling).start()
    remote(items.at[other], items.at[other], it_send.at[0], it_recv.at[0], sibling).wait_recv()
    remote(shifts.at[other], shifts.at[other], it_send.at[1], it_recv.at[1], sibling).wait_recv()
    for side in range(2):
        items_t[:, pl.ds(side * half, half)] = items[side].T

    row_ids = lax.broadcasted_iota(jnp.int32, (half, rows), 0)
    base = col * (2 * half)

    def score_chunk(c):
        tops = []
        picks = []
        for side in range(2):
            product = lax.dot_general(
                items[side], q_all[c], (((1,), (1,)), ((), ())), preferred_element_type=jnp.float32
            )
            shift = shifts[side][:, None, :, :]
            value = (logit_scale * product).reshape(slots, BLOCK // 8, 8, rows) - shift
            value = value.reshape(half, rows)
            scores[c, side] = value
            marked = row_ids == t_all[c][0:1, :] - (base + side * half)
            tops.append(jnp.max(value, axis=0, keepdims=True))
            picks.append(jnp.sum(jnp.where(marked, value, 0.0), axis=0, keepdims=True))
        top = jnp.maximum(tops[0], tops[1])
        total = jnp.zeros((1, rows), jnp.float32)
        for side in range(2):
            total = total + jnp.sum(jnp.exp(scores[c, side] - top), axis=0, keepdims=True)
        stats[col, pl.ds(c, 1), :] = top
        stats[col, pl.ds(n_col + c, 1), :] = total
        pick_own[c] = jnp.broadcast_to(picks[0] + picks[1], (8, rows))

    load_own.wait()
    score_chunk(col)

    @pl.loop(1, n_col)
    def _(step):
        c = (col + step) % n_col
        remote(q_all.at[c], q_all.at[c], q_send.at[c], q_recv.at[c], sibling).wait_recv()
        remote(t_all.at[c], t_all.at[c], t_send.at[c], t_recv.at[c], sibling).wait_recv()
        score_chunk(c)

    for step in range(1, n_col):
        c = (col + step) % n_col
        remote(stats.at[col], stats.at[col], st_send.at[c], st_recv.at[col], column(c)).start()
    for step in range(1, n_col):
        c = (col + step) % n_col
        remote(pick_own.at[c], pick_all.at[col], pk_send.at[c], pk_recv.at[col], column(c)).start()
    for step in range(1, n_col):
        c = (col + step) % n_col
        remote(stats.at[c], stats.at[c], st_send.at[c], st_recv.at[c], sibling).wait_recv()

    top = stats[0, 0:n_col, :]
    for c in range(1, n_col):
        top = jnp.maximum(top, stats[c, 0:n_col, :])
    total = jnp.zeros_like(top)
    for c in range(n_col):
        total = total + stats[c, n_col : 2 * n_col, :] * jnp.exp(stats[c, 0:n_col, :] - top)
    norm[...] = top + jnp.log(total)

    every_query = q_all[...].reshape(n_col * rows, width)

    slot_rows = lax.broadcasted_iota(jnp.int32, (BLOCK, rows), 0)

    def item_part(side, j):
        @pl.loop(0, n_col)
        def _(c):
            marked = slot_rows == t_all[c][0:1, :] - (base + side * half + j * BLOCK)
            probs = jnp.exp(scores[c, side, pl.ds(j * BLOCK, BLOCK), :] - norm[pl.ds(c, 1), :])
            value = (probs - marked.astype(jnp.float32)).astype(jnp.bfloat16)
            dlog[side, pl.ds(j * BLOCK, BLOCK), pl.ds(pl.multiple_of(c * rows, rows), rows)] = value

        return logit_scale * jnp.dot(
            dlog[side, pl.ds(j * BLOCK, BLOCK), :], every_query, preferred_element_type=jnp.float32
        )

    def to_sibling(j):
        where = pl.ds(j * BLOCK, BLOCK)
        return remote(part_out.at[where, :], part_in.at[where, :], gp_send.at[j], gp_recv.at[j], sibling)

    for j in range(slots):
        part_out[pl.ds(j * BLOCK, BLOCK), :] = item_part(other, j).astype(jnp.bfloat16)
        to_sibling(j).start()
    for j in range(slots):
        part_own[pl.ds(j * BLOCK, BLOCK), :] = item_part(core, j)

    def query_part(c):
        lanes = pl.ds(pl.multiple_of(c * rows, rows), rows)
        value = jnp.dot(items_t[:, pl.ds(0, half)], dlog[0, :, lanes], preferred_element_type=jnp.float32)
        value += jnp.dot(items_t[:, pl.ds(half, half)], dlog[1, :, lanes], preferred_element_type=jnp.float32)
        return logit_scale * value

    @pl.loop(1, n_col)
    def _(step):
        c = (col + step) % n_col
        qg_out[c] = query_part(c).astype(jnp.bfloat16)
        remote(qg_out.at[c], qg_in.at[col], qg_send.at[c], qg_recv.at[col], column(c)).start()

    def exchange_slot(h, j):
        where = pl.ds(j * BLOCK, BLOCK)
        return remote(
            s_out.at[h, where, :], s_in.at[h, where, :], ss_send.at[h, j], ss_recv.at[h, j], flipped(h % bits)
        )

    for j in range(slots):
        where = pl.ds(j * BLOCK, BLOCK)
        to_sibling(j).wait_recv()
        value = part_own[where, :] + part_in[where, :].astype(jnp.float32)
        for h in range(2):
            s_out[h, where, :] = value[:, h * half_width : (h + 1) * half_width].astype(jnp.bfloat16)
            exchange_slot(h, j).start()

    def exchange(stage, h, g):
        where = pl.ds(g * group, group)
        return remote(
            bf_out.at[stage - 1, h, where, :], bf_in.at[stage - 1, h, where, :],
            bf_send.at[stage - 1, h, g], bf_recv.at[stage - 1, h, g], flipped((stage + h) % bits),
        )

    def pass_on(stage, h, g, value):
        if stage < bits:
            bf_out[stage - 1, h, pl.ds(g * group, group), :] = value.astype(jnp.bfloat16)
            exchange(stage, h, g).start()
        else:
            grad_ref[pl.ds(g * group, group), pl.ds(h * half_width, half_width)] = value

    qg_own[...] = query_part(col)
    for h in range(2):
        announce(h).wait_recv()
        for j in range(slots):
            exchange_slot(h, j).wait_recv()
    for g in range(groups):
        for h in range(2):
            pieces = []
            for b in range(g * group // BLOCK, (g + 1) * group // BLOCK):
                mine = jnp.zeros((BLOCK // 8, 8, half_width), jnp.float32)
                theirs = mine
                for j in range(slots):
                    where = pl.ds(j * BLOCK, BLOCK)
                    mine = mine + is_block(id_own[j], b) * tiles(s_out[h, where, :])
                    theirs = theirs + is_block(id_in[h, j], b) * tiles(s_in[h, where, :])
                pieces.append((mine + theirs).reshape(BLOCK, half_width))
            pass_on(1, h, g, jnp.concatenate(pieces, axis=0))

    total_qg = qg_own[...]
    picked = pick_own[col]
    for step in range(1, n_col):
        c = (col + step) % n_col
        remote(qg_in.at[c], qg_in.at[c], qg_send.at[c], qg_recv.at[c], sibling).wait_recv()
        remote(pick_all.at[c], pick_all.at[c], pk_send.at[c], pk_recv.at[c], sibling).wait_recv()
        total_qg = total_qg + qg_in[c].astype(jnp.float32)
        picked = picked + pick_all[c]
    qgrad_ref[0] = total_qg.T
    loss_ref[...] = norm[pl.ds(col, 1), :] - picked[0:1, :]

    for stage in range(1, bits):
        for g in range(groups):
            for h in range(2):
                where = pl.ds(g * group, group)
                exchange(stage, h, g).wait_recv()
                value = bf_out[stage - 1, h, where, :].astype(jnp.float32)
                value = value + bf_in[stage - 1, h, where, :].astype(jnp.float32)
                pass_on(stage + 1, h, g, value)

    for step in range(1, n_col):
        c = (col + step) % n_col
        remote(q_all.at[col], q_all.at[col], q_send.at[c], q_recv.at[c], sibling).wait_send()
        remote(t_all.at[col], t_all.at[col], t_send.at[c], t_recv.at[c], sibling).wait_send()
        remote(stats.at[col], stats.at[col], st_send.at[c], st_recv.at[c], sibling).wait_send()
        remote(pick_own.at[c], pick_own.at[c], pk_send.at[c], pk_recv.at[c], sibling).wait_send()
        remote(qg_out.at[c], qg_out.at[c], qg_send.at[c], qg_recv.at[c], sibling).wait_send()
    remote(items.at[core], items.at[core], it_send.at[0], it_recv.at[0], sibling).wait_send()
    remote(shifts.at[core], shifts.at[core], it_send.at[1], it_recv.at[1], sibling).wait_send()
    for j in range(slots):
        to_sibling(j).wait_send()
    for h in range(2):
        announce(h).wait_send()
        for j in range(slots):
            exchange_slot(h, j).wait_send()
        for stage in range(1, bits):
            for g in range(groups):
                exchange(stage, h, g).wait_send()


def local(n_rep, n_shard, queries, targets, samp_ids, counts, logq, table, first_moment, second_moment):
    rows, width = queries.shape[1:]
    slots = samp_ids.shape[1]
    items_held = table.shape[0]
    blocks = items_held // BLOCK
    n_col = n_shard // 2
    bits = n_rep.bit_length() - 1
    half = slots * BLOCK
    f32, bf16 = jnp.float32, jnp.bfloat16
    dma = pltpu.SemaphoreType.DMA
    vmem = pl.BlockSpec(memory_space=pltpu.VMEM)
    pair_flops = n_col * rows * 2 * half * width
    own_loss, query_grad, gradient = pl.pallas_call(
        functools.partial(kernel, n_rep, n_col, slots, blocks),
        out_shape=(
            jax.ShapeDtypeStruct((1, rows), f32),
            jax.ShapeDtypeStruct((1, rows, width), f32),
            jax.ShapeDtypeStruct((items_held, width), f32),
        ),
        in_specs=[pl.BlockSpec(memory_space=pltpu.HBM)] * 6,
        out_specs=(vmem, vmem, vmem),
        scratch_shapes=[
            pltpu.SMEM((1, slots), jnp.int32),
            pltpu.SMEM((1, 1), jnp.int32),
            pltpu.SMEM((1, slots), f32),
            pltpu.VMEM((1, rows), jnp.int32),
            pltpu.VMEM((items_held, width), f32),
            pltpu.VMEM((slots, 8, BLOCK), f32),
            pltpu.VMEM((2, slots, 8, BLOCK), f32),
            pltpu.VMEM((2, half, width // 2), bf16),
            pltpu.VMEM((2, half, width // 2), bf16),
            pltpu.VMEM((n_col, rows, width), bf16),
            pltpu.VMEM((n_col, 8, rows), jnp.int32),
            pltpu.VMEM((2, half, width), bf16),
            pltpu.VMEM((width, 2 * half), bf16),
            pltpu.VMEM((2, slots, 8, BLOCK), f32),
            pltpu.VMEM((n_col, 2, half, rows), f32),
            pltpu.VMEM((2, half, n_col * rows), bf16),
            pltpu.VMEM((n_col, 2 * n_col, rows), f32),
            pltpu.VMEM((n_col, rows), f32),
            pltpu.VMEM((n_col, 8, rows), f32),
            pltpu.VMEM((n_col, 8, rows), f32),
            pltpu.VMEM((half, width), f32),
            pltpu.VMEM((half, width), bf16),
            pltpu.VMEM((half, width), bf16),
            pltpu.VMEM((width, rows), f32),
            pltpu.VMEM((n_col, width, rows), bf16),
            pltpu.VMEM((n_col, width, rows), bf16),
            pltpu.VMEM((max(bits - 1, 1), 2, items_held, width // 2), bf16),
            pltpu.VMEM((max(bits - 1, 1), 2, items_held, width // 2), bf16),
            dma((4,)), dma(()), dma(()), dma((2,)), dma((2,)), dma((2, slots)), dma((2, slots)),
            dma((n_col,)), dma((n_col,)), dma((n_col,)), dma((n_col,)),
            dma((2,)), dma((2,)),
            dma((n_col,)), dma((n_col,)), dma((n_col,)), dma((n_col,)),
            dma((slots,)), dma((slots,)),
            dma((n_col,)), dma((n_col,)),
            dma((bits, 2, blocks)), dma((bits, 2, blocks)),
        ],
        compiler_params=pltpu.CompilerParams(
            collective_id=0, has_side_effects=True, vmem_limit_bytes=60 * 1024 * 1024
        ),
        cost_estimate=pl.CostEstimate(
            flops=6 * pair_flops, bytes_accessed=4 * items_held * width, transcendentals=2 * pair_flops // width
        ),
    )(samp_ids, counts, logq, targets, queries, table)
    tile = items_held // (2 if blocks % 2 == 0 else 1)
    by_tile = pl.BlockSpec((tile, width), lambda i: (i, 0))
    loss_spec = pl.BlockSpec((1, rows), lambda i: (0, 0))
    qgrad_spec = pl.BlockSpec((1, rows, width), lambda i: (0, 0, 0))
    held = jax.ShapeDtypeStruct((items_held, width), f32)
    return pl.pallas_call(
        finish_kernel,
        grid=(items_held // tile,),
        out_shape=(
            jax.ShapeDtypeStruct((1, rows), f32),
            jax.ShapeDtypeStruct((1, rows, width), f32),
            held, held, held,
        ),
        in_specs=[loss_spec, qgrad_spec, by_tile, by_tile, by_tile, by_tile],
        out_specs=(loss_spec, qgrad_spec, by_tile, by_tile, by_tile),
        compiler_params=pltpu.CompilerParams(vmem_limit_bytes=60 * 1024 * 1024),
    )(own_loss, query_grad, gradient, table, first_moment, second_moment)


def solution(mesh):
    in_specs = (
        P("rep", "shard", None),
        P("rep", "shard"),
        P("rep", "shard"),
        P("rep", "shard"),
        P("rep", "shard"),
        P("shard", None),
        P("shard", None),
        P("shard", None),
    )
    out_specs = (
        P("rep", "shard"),
        P("rep", "shard", None),
        P("shard", None),
        P("shard", None),
        P("shard", None),
    )
    step = functools.partial(local, mesh.shape["rep"], mesh.shape["shard"])
    return jax.shard_map(step, mesh=mesh, in_specs=in_specs, out_specs=out_specs, check_vma=False)
```
